32 devices in a mesh: segment: 4 (over y, x), tensor: 8 (over z, core).
Axes of the slice: x: 2, y: 2, z: 4, core: 2. Of those that a mesh axis runs over, the one named last changes fastest.
Arguments:
- tokens: int32 [192], replicated, may hold values from 0 to 64127
- embedding: bfloat16 [64128, 4096], P('segment', 'tensor'), may hold values from -36 to 36
- gain: float32 [2, 4096], replicated, may hold values from 0.1 to 1.9
- gate_weight: bfloat16 [4, 4096, 7168], P('segment', None, 'tensor'), may hold values from -0.09375 to 0.09375
- down_weight: bfloat16 [4, 7168, 4096], P('segment', 'tensor'), may hold values from -0.0625 to 0.0625
- basis: bfloat16 [4096, 512], P('tensor'), may hold values from -0.09375 to 0.09375
Outputs:
- collected: bfloat16 [4, 192, 512], P('segment')
The draws below stay inside these ranges and needn't reach their ends.
All inputs are finite; a program needn't handle non-finite values.
Results may differ from the reference program's by a relative error of at most 0.02.
Values may be sent and summed in bfloat16 or wider, within the bound.
No kernel may reach another device: no remote copies, remote signals or barrier semaphores. Data moves between devices by JAX's collectives and lax.ppermute only.
A program may use at most 128 MiB of HBM per device.

```python
import math
import jax
import jax.numpy as jnp
import numpy as np
from jax import lax

D = 4096
FF = 14336
R = 512
VOCAB = 64128
SECTIONS = 2
BLOCKS = 16
TOKENS = 192
N_SEGMENT = 4


def draw_embedding(key, part):
    key = jax.random.fold_in(key, 7)
    row_key, column_key, base_key = jax.random.split(key, 3)
    row_scale = jnp.exp(jax.random.uniform(row_key, (VOCAB, 1), jnp.float32, math.log(0.3), math.log(3.0)))
    column_scale = jnp.exp(jax.random.uniform(column_key, (1, D), jnp.float32, math.log(0.3), math.log(3.0)))
    base = jnp.clip(jax.random.normal(base_key, (VOCAB, D), jnp.float32), -4.0, 4.0)
    return (base * row_scale * column_scale).astype(jnp.bfloat16)


def place_ends(entries, stream_key, least, top_value):
    shape = entries.shape
    index_at = [jax.random.randint(jax.random.fold_in(stream_key, axis), (), 0, shape[axis]) for axis in range(len(shape))]
    entries = entries.at[tuple(index_at)].set(least)
    longest = shape.index(max(shape))
    index_at[longest] = (index_at[longest] + 1) % shape[longest]
    return entries.at[tuple(index_at)].set(top_value)


def raised(entries, stream_key, source, target, parts, factor):
    owner, partner = [(jnp.arange(entries.shape[axis_at]) // (entries.shape[axis_at] // parts)).reshape([-1 if axis == axis_at else 1 for axis in range(entries.ndim)]) for axis_at in (source, target)]
    chosen = jax.random.permutation(stream_key, parts)[partner]
    strong = (owner == chosen) | (owner == (partner + parts // 2) % parts)
    return jnp.where(strong, factor * entries, entries)


def shard_levels(own_key, dims, shards, least, high):
    factor_of = 1.0
    for axis_at, shards_of in shards:
        heights = jax.random.uniform(jax.random.fold_in(jax.random.fold_in(own_key, 6), axis_at), (shards_of,), jnp.float32, least / len(shards), high / len(shards))
        factor_of = factor_of * jnp.repeat(jnp.exp(heights), dims[axis_at] // shards_of).reshape((-1,) + (1,) * (len(dims) - 1 - axis_at))
    return factor_of


def rank_bounds(amount, lean):
    loads = [(1 << 20) // math.isqrt(standing ** lean) + 1 for standing in range(1, amount + 1)]
    scale = 1 + sum(loads) // (1 << 30)
    return np.cumsum(np.array([max(1, weight // scale) for weight in loads]))


def ranked_ids(rng, dims, amount, skew):
    listing = rank_bounds(amount, skew)
    ticket = jax.random.randint(jax.random.fold_in(rng, 1), dims, 0, int(listing[amount - 1]))
    standing = jnp.searchsorted(jnp.asarray(listing, jnp.int32), ticket, side="right")
    return jax.random.permutation(jax.random.fold_in(rng, 2), amount)[standing].astype(jnp.int32)


def bell_draw(key, dims, scale, most, pieces=(), dtype=jnp.bfloat16):
    drawn = scale * jax.random.normal(key, dims, jnp.float32)
    if pieces:
        drawn = drawn * shard_levels(key, dims, pieces, -0.22, 0.18)
    return jnp.clip(drawn, -most, most).astype(dtype)


def bell_draw_with(rng, extent, scale, limit, cuts, heavy, kind=jnp.bfloat16):
    entries = scale * jax.random.normal(rng, extent, jnp.float32)
    if cuts:
        entries = entries * shard_levels(rng, extent, cuts, -0.22, 0.18)
    return jnp.clip(raised(entries, jax.random.fold_in(rng, 3), *heavy), -limit, limit).astype(kind)


def setup_inputs(seed: int = 0) -> dict:
    arg_keys = jax.random.split(jax.random.key(seed), 7)
    tokens = place_ends(ranked_ids(arg_keys[0], (TOKENS,), VOCAB, 2), jax.random.fold_in(arg_keys[0], 3), 0, VOCAB - 1).astype(jnp.int32)
    embedding = draw_embedding(jax.random.fold_in(arg_keys[6], 71), 0)
    gain = jnp.clip(1.0 + 0.18 * jax.random.normal(arg_keys[2], (SECTIONS, D), jnp.float32), 0.1, 1.9)
    gate_weight = bell_draw(arg_keys[3], (N_SEGMENT, D, FF // 2), D ** -0.5, 0.09375, ((0, 4), (2, 8)))
    down_weight = bell_draw_with(arg_keys[4], (N_SEGMENT, FF // 2, D), FF ** -0.5, 0.0625, ((0, 4), (1, 8)), (1, 2, 8, 2.0))
    basis = bell_draw(arg_keys[5], (D, R), D ** -0.5, 0.09375, ((0, 8),))
    return {"tokens": tokens, "embedding": embedding, "gain": gain, "gate_weight": gate_weight, "down_weight": down_weight, "basis": basis}


def reference(tokens, embedding, gain, gate_weight, down_weight, basis):
    embedded = jnp.take(embedding, tokens, axis=0)
    embed_wide = embedded.astype(jnp.float32)
    basis_wide = basis.astype(jnp.float32)
    width = FF // BLOCKS
    outputs = []
    carried = embedded
    for section in range(SECTIONS):
        if section == 0:
            layer_input = embedded
        else:
            layer_input = (jnp.dot(carried, basis.T, preferred_element_type=jnp.float32) + embed_wide).astype(jnp.bfloat16)
        wide_input = layer_input.astype(jnp.float32)
        inverse_norm = lax.rsqrt(lax.optimization_barrier(jnp.mean(wide_input * wide_input, axis=1, keepdims=True)) + 1e-05)
        scaled = (wide_input * gain[section][None, :]).astype(jnp.bfloat16)
        gate_full = jnp.concatenate([gate_weight[2 * section], gate_weight[2 * section + 1]], axis=1)
        down_full = jnp.concatenate([down_weight[2 * section], down_weight[2 * section + 1]], axis=0)
        activation = jax.nn.silu(inverse_norm * jnp.dot(scaled, gate_full, preferred_element_type=jnp.float32)).astype(jnp.bfloat16)
        hidden_blocks = activation.reshape(TOKENS, BLOCKS, width).transpose(1, 0, 2)
        down_blocks = down_full.reshape(BLOCKS, width, D)

        def add_block(total, operands):
            hidden_block, down_block = operands
            term = jnp.dot(hidden_block, down_block, preferred_element_type=jnp.float32).astype(jnp.bfloat16)
            term = lax.optimization_barrier(term)
            return (total + term.astype(jnp.float32), None)
        summed, _ = lax.scan(add_block, jnp.zeros((TOKENS, D), jnp.float32), (hidden_blocks, down_blocks))
        update = wide_input - embed_wide + summed
        coefficients = jnp.dot(update, basis_wide, precision=lax.Precision.HIGHEST).astype(jnp.bfloat16)
        outputs.append(coefficients)
        outputs.append(coefficients)
        carried = coefficients
    return jnp.stack(outputs)
```

```python
import functools

import jax
import jax.numpy as jnp
from jax import lax
from jax.experimental import pallas as pl
from jax.experimental.pallas import tpu as pltpu
from jax.sharding import PartitionSpec as P

EPSILON = 1e-05
GROUP = 4
TILE = 16
CHUNK = 512
F32 = jnp.float32
BF16 = jnp.bfloat16


def swap(value, axis, mask):
    return lax.ppermute(value, axis, [(i, i ^ mask) for i in range(lax.axis_size(axis))])


def onward(value, flip):
    size = lax.axis_size("segment")
    return lax.ppermute(value, "segment", [(i, (i ^ flip) + 2) for i in range(size - 2)])


def tree_sum(values):
    while len(values) > 1:
        values = [values[i] + values[i + 1] for i in range(0, len(values), 2)]
    return values[0]


def fetch_kernel(block_rows, vocab, tokens_smem, tokens_row, table, *refs):
    outs, buffer, sem = refs[:GROUP], refs[GROUP], refs[GROUP + 1]
    segment = lax.axis_index("segment")
    low = segment * vocab
    count = GROUP * block_rows

    def start(i, carry):
        local = jnp.clip(tokens_smem[i] - low, 0, vocab - 1)
        first = pl.multiple_of((local // TILE) * TILE, TILE)
        place = pl.multiple_of(i * TILE, TILE)
        pltpu.make_async_copy(
            table.at[pl.ds(first, TILE), :], buffer.at[pl.ds(place, TILE), :], sem
        ).start()
        return carry

    lax.fori_loop(0, count, start, 0, unroll=8)
    wanted = tokens_row[...] - low
    inside = (wanted >= 0) & (wanted < vocab)
    code = jnp.where(inside, lax.rem(wanted, TILE), TILE)
    rows = lax.broadcasted_iota(jnp.int32, (count, count), 0)
    columns = lax.broadcasted_iota(jnp.int32, (count, count), 1)
    code_column = jnp.sum(jnp.where(rows == columns, code, 0), axis=1, keepdims=True)
    pltpu.make_async_copy(buffer, buffer, sem).wait()
    home = lax.rem(segment, GROUP)
    wide = block_rows * TILE
    row_of = lax.broadcasted_iota(jnp.int32, (block_rows, wide), 0)
    lane_of = lax.broadcasted_iota(jnp.int32, (block_rows, wide), 1)
    results = []
    for block in range(GROUP):
        code_block = code_column[block * block_rows : (block + 1) * block_rows]
        hot = (lane_of == row_of * TILE + code_block) & (code_block < TILE)
        hot = jnp.where(hot, 1.0, 0.0).astype(BF16)
        results.append(
            jnp.dot(
                hot, buffer[block * wide : (block + 1) * wide, :], preferred_element_type=F32
            ).astype(BF16)
        )
    for block in range(GROUP):
        for mask in range(GROUP):

            @pl.when(jnp.bitwise_xor(home, mask) == block)
            def _(block=block, mask=mask):
                outs[mask][...] = results[block]


def fetch_rows(tokens, embedding):
    vocab, features = embedding.shape
    block_rows = tokens.shape[0] // GROUP
    if vocab % TILE:
        segment = lax.axis_index("segment")
        local = tokens - segment * vocab
        inside = (local >= 0) & (local < vocab)
        picked = jnp.take(embedding, jnp.clip(local, 0, vocab - 1), axis=0)
        picked = jnp.where(inside[:, None], picked, jnp.zeros_like(picked))
        picked = picked.reshape(GROUP, block_rows, features)
        home = segment % GROUP
        return [lax.dynamic_index_in_dim(picked, home ^ m, 0, False) for m in range(GROUP)]
    return pl.pallas_call(
        functools.partial(fetch_kernel, block_rows, vocab),
        out_shape=[jax.ShapeDtypeStruct((block_rows, features), BF16)] * GROUP,
        in_specs=[
            pl.BlockSpec(memory_space=pltpu.SMEM),
            pl.BlockSpec(memory_space=pltpu.VMEM),
            pl.BlockSpec(memory_space=pl.ANY),
        ],
        out_specs=[pl.BlockSpec(memory_space=pltpu.VMEM)] * GROUP,
        scratch_shapes=[
            pltpu.VMEM((tokens.shape[0] * TILE, features), BF16),
            pltpu.SemaphoreType.DMA,
        ],
        compiler_params=pltpu.CompilerParams(vmem_limit_bytes=32 * 2**20),
        name="fetch_rows",
    )(tokens, tokens.reshape(1, -1), embedding)


def section_kernel(first, chips, *refs):
    if first:
        pieces, refs = refs[: 2 * GROUP], refs[2 * GROUP :]
    else:
        (half_own, half_other, embedded), refs = refs[:3], refs[3:]
    (gain, gate, down, basis), refs = refs[:4], refs[4:]
    (own, send), refs = refs[:2], refs[2:]
    if first:
        embedded, refs = refs[0], refs[1:]
    gates, downs, bases, total, projected, sems = refs
    tokens, width = embedded.shape
    segment = lax.axis_index("segment")
    place = lax.axis_index("tensor")
    core = lax.rem(place, 2)
    chip = place // 2
    chunks = width // CHUNK

    def gate_copy(k):
        return pltpu.make_async_copy(gate.at[0, pl.ds(k * CHUNK, CHUNK), :], gates.at[k], sems.at[0, k])

    def down_copy(k):
        return pltpu.make_async_copy(down.at[0, :, pl.ds(k * CHUNK, CHUNK)], downs.at[k], sems.at[1, k])

    def basis_copy(k):
        return pltpu.make_async_copy(basis.at[pl.ds(k * CHUNK, CHUNK), :], bases.at[k], sems.at[2, k])

    if first:
        order = [gate_copy, down_copy, basis_copy]
        for copy in order:
            for k in range(chunks):
                copy(k).start()
        features = width // (2 * chips)
        rows = tokens // GROUP
        home = lax.rem(segment, GROUP)
        for side in range(2):
            for block in range(GROUP):
                row = pl.multiple_of(jnp.bitwise_xor(home, block) * rows, rows)
                for turn in range(chips):
                    column = (jnp.bitwise_xor(chip, turn) * 2 + jnp.bitwise_xor(core, side)) * features
                    embedded[pl.ds(row, rows), pl.ds(pl.multiple_of(column, features), features)] = (
                        pieces[side * GROUP + block][turn]
                    )
    else:
        for k in range(chunks):
            basis_copy(k).start()
            gate_copy(k).start()
        for k in range(chunks):
            down_copy(k).start()
        half = tokens // 2
        flipped = jnp.where(core == 0, half_own[...], half_other[...])
        second = jnp.where(core == 0, half_other[...], half_own[...])
        received = jnp.concatenate([flipped, second], axis=0)

    gain_row = gain[pl.ds(segment // 2, 1), :]
    squares = jnp.zeros((tokens, 1), F32)
    for k in range(chunks):
        span = slice(k * CHUNK, (k + 1) * CHUNK)
        if first:
            wide = embedded[:, span].astype(F32)
        else:
            basis_copy(k).wait()
            expanded = lax.dot_general(
                received, bases[k], (((1,), (1,)), ((), ())), preferred_element_type=F32
            )
            wide = (expanded + embedded[:, span].astype(F32)).astype(BF16).astype(F32)
        squares = squares + jnp.sum(wide * wide, axis=1, keepdims=True)
        scaled = (wide * gain_row[:, span]).astype(BF16)
        gate_copy(k).wait()
        product = jnp.dot(scaled, gates[k], preferred_element_type=F32)
        total[...] = product if k == 0 else total[...] + product
    inverse_norm = lax.rsqrt(squares / width + EPSILON)
    activation = jax.nn.silu(total[...] * inverse_norm).astype(BF16)

    if first:
        projected[...] = jnp.zeros_like(projected)
    else:
        share = width // (2 * chips)
        at = pl.multiple_of(place * share, share)
        table = bases[place * share // CHUNK]
        table = bases.at[place * share // CHUNK][
            pl.ds(pl.multiple_of(lax.rem(place * share, CHUNK), share), share), :
        ]
        expanded = lax.dot_general(
            received, table, (((1,), (1,)), ((), ())), preferred_element_type=F32
        )
        base = embedded[:, pl.ds(at, share)].astype(F32)
        difference = (expanded + base).astype(BF16).astype(F32) - base
        coarse = difference.astype(BF16)
        fine = (difference - coarse.astype(F32)).astype(BF16)
        term = jnp.dot(coarse, table, preferred_element_type=F32) + jnp.dot(
            fine, table, preferred_element_type=F32
        )
        projected[...] = jnp.where(lax.rem(segment, 2) == 0, term, jnp.zeros_like(term))
    for k in range(chunks):
        down_copy(k).wait()
        partial = jnp.dot(activation, downs[k], preferred_element_type=F32).astype(BF16)
        if first:
            basis_copy(k).wait()
        projected[...] += jnp.dot(partial, bases[k], preferred_element_type=F32)
    half = tokens // 2
    own[...] = projected[pl.ds(pl.multiple_of(core * half, half), half), :].astype(BF16)
    send[...] = projected[pl.ds(pl.multiple_of((1 - core) * half, half), half), :].astype(BF16)


def run_section(first, inputs, gain, gate, down, basis, tokens):
    width, rank = basis.shape
    hidden = gate.shape[2]
    chunks = width // CHUNK
    halves = [jax.ShapeDtypeStruct((tokens // 2, rank), BF16)] * 2
    outs = halves + ([jax.ShapeDtypeStruct((tokens, width), BF16)] if first else [])
    vmem = pl.BlockSpec(memory_space=pltpu.VMEM)
    anywhere = pl.BlockSpec(memory_space=pl.ANY)
    return pl.pallas_call(
        functools.partial(section_kernel, first, lax.axis_size("tensor") // 2),
        out_shape=outs,
        in_specs=[vmem] * (len(inputs) + 1) + [anywhere] * 3,
        out_specs=[vmem] * len(outs),
        scratch_shapes=[
            pltpu.VMEM((chunks, CHUNK, hidden), BF16),
            pltpu.VMEM((chunks, hidden, CHUNK), BF16),
            pltpu.VMEM((chunks, CHUNK, rank), BF16),
            pltpu.VMEM((tokens, hidden), F32),
            pltpu.VMEM((tokens, rank), F32),
            pltpu.SemaphoreType.DMA((3, chunks)),
        ],
        compiler_params=pltpu.CompilerParams(vmem_limit_bytes=48 * 2**20),
        cost_estimate=pl.CostEstimate(
            flops=2 * tokens * width * (2 * hidden + rank),
            bytes_accessed=2 * width * (2 * hidden + rank),
            transcendentals=tokens * hidden,
        ),
        name="section_first" if first else "section_next",
    )(*inputs, gain, gate, down, basis)


def per_device(tokens, embedding, gain, gate_weight, down_weight, basis):
    segments = lax.axis_size("segment")
    chips = lax.axis_size("tensor") // 2
    sections = segments // 2
    section = lax.axis_index("segment") // 2
    core = lax.axis_index("tensor") % 2
    count = tokens.shape[0]
    whole_basis = lax.all_gather(basis, "tensor", axis=0, tiled=True)

    blocks = fetch_rows(tokens, embedding)
    mask = GROUP
    while mask < segments:
        blocks = [block + swap(block, "segment", mask) for block in blocks]
        mask *= 2
    complete = tree_sum(
        [block if m == 0 else swap(block, "segment", m) for m, block in enumerate(blocks)]
    )
    along = jnp.stack([complete] + [swap(complete, "tensor", 2 * m) for m in range(1, chips)])
    mine = [along] + [swap(along, "segment", m) for m in range(1, GROUP)]
    theirs = [swap(piece, "tensor", 1) for piece in mine]

    received = embedded = None
    kept = None
    for step in range(sections):
        if step == 0:
            own, send, embedded = run_section(
                True, mine + theirs, gain, gate_weight, down_weight, whole_basis, count
            )
        else:
            own, send = run_section(
                False, [*received, embedded], gain, gate_weight, down_weight, whole_basis, count
            )
        chip_sum = (own.astype(F32) + swap(send, "tensor", 1).astype(F32)).astype(BF16)
        terms = [chip_sum] + [swap(chip_sum, "tensor", 2 * m) for m in range(1, chips)]
        half_sum = tree_sum([term.astype(F32) for term in terms]).astype(BF16)
        result = half_sum.astype(F32) + swap(half_sum, "segment", 1).astype(F32)
        if step + 1 < sections:
            handed = onward(half_sum, 0).astype(F32) + onward(half_sum, 1).astype(F32)
            result = jnp.where(section <= step, result, handed)
        result = result.astype(BF16)
        received = (result, swap(result, "tensor", 1))
        if step == 0:
            kept = received
        else:
            kept = tuple(jnp.where(section == step, new, old) for new, old in zip(received, kept))
    near, far = kept
    first = jnp.where(core == 0, near, far)
    second = jnp.where(core == 0, far, near)
    return jnp.concatenate([first, second], axis=0)[None]


def solution(mesh):
    placed = (
        P(),
        P("segment", "tensor"),
        P(),
        P("segment", None, "tensor"),
        P("segment", "tensor", None),
        P("tensor", None),
    )
    return jax.shard_map(
        per_device, mesh=mesh, in_specs=placed, out_specs=P("segment", None, None), check_vma=False
    )
```

```python
import functools

import jax
import jax.numpy as jnp
from jax import lax
from jax.experimental import pallas as pl
from jax.experimental.pallas import tpu as pltpu
from jax.sharding import PartitionSpec as P

EPSILON = 1e-05
GROUP = 4
TILE = 16
PARTS = 8
CHUNK = 512
F32 = jnp.float32
BF16 = jnp.bfloat16


def swap(value, axis, mask):
    return lax.ppermute(value, axis, [(i, i ^ mask) for i in range(lax.axis_size(axis))])


def onward(value, flip):
    size = lax.axis_size("segment")
    return lax.ppermute(value, "segment", [(i, (i ^ flip) + 2) for i in range(size - 2)])


def tree_sum(values):
    while len(values) > 1:
        values = [values[i] + values[i + 1] for i in range(0, len(values), 2)]
    return values[0]


def split_copies(source, target, sems):
    rows = source.shape[0]
    parts = max(p for p in range(1, PARTS + 1) if rows % (TILE * p) == 0)
    size = rows // parts
    return [
        pltpu.make_async_copy(
            source.at[pl.ds(k * size, size), :], target.at[pl.ds(k * size, size), :], sems.at[k]
        )
        for k in range(parts)
    ]


def fetch_kernel(block_rows, vocab, tokens_smem, tokens_row, table, gate, down, *refs):
    outs, (near_gate, near_down, buffer, sems, weight_sems) = refs[:GROUP], refs[GROUP:]
    weights = split_copies(gate.at[0], near_gate, weight_sems.at[0])
    weights += split_copies(down.at[0], near_down, weight_sems.at[1])
    segment = lax.axis_index("segment")
    low = segment * vocab
    count = GROUP * block_rows

    def held(i):
        local = tokens_smem[i] - low
        return local, (local >= 0) & (local < vocab)

    def copy(i, local):
        first = pl.multiple_of((local // TILE) * TILE, TILE)
        place = pl.multiple_of(i * TILE, TILE)
        return pltpu.make_async_copy(
            table.at[pl.ds(first, TILE), :], buffer.at[pl.ds(place, TILE), :], sems.at[i]
        )

    def start(i, carry):
        local, here = held(i)

        @pl.when(here)
        def _():
            copy(i, local).start()

        return carry

    def finish(i, carry):
        local, here = held(i)

        @pl.when(here)
        def _():
            copy(i, local).wait()

        return carry

    buffer[...] = jnp.zeros_like(buffer)
    lax.fori_loop(0, count, start, 0, unroll=8)
    for weight in weights:
        weight.start()
    wanted = tokens_row[...] - low
    inside = (wanted >= 0) & (wanted < vocab)
    code = jnp.where(inside, lax.rem(wanted, TILE), TILE)
    rows = lax.broadcasted_iota(jnp.int32, (count, count), 0)
    columns = lax.broadcasted_iota(jnp.int32, (count, count), 1)
    code_column = jnp.sum(jnp.where(rows == columns, code, 0), axis=1, keepdims=True)
    lax.fori_loop(0, count, finish, 0, unroll=8)
    home = lax.rem(segment, GROUP)
    wide = block_rows * TILE
    row_of = lax.broadcasted_iota(jnp.int32, (block_rows, wide), 0)
    lane_of = lax.broadcasted_iota(jnp.int32, (block_rows, wide), 1)
    results = []
    for block in range(GROUP):
        code_block = code_column[block * block_rows : (block + 1) * block_rows]
        hot = (lane_of == row_of * TILE + code_block) & (code_block < TILE)
        hot = jnp.where(hot, 1.0, 0.0).astype(BF16)
        results.append(
            jnp.dot(
                hot, buffer[block * wide : (block + 1) * wide, :], preferred_element_type=F32
            ).astype(BF16)
        )
    for block in range(GROUP):
        for mask in range(GROUP):

            @pl.when(jnp.bitwise_xor(home, mask) == block)
            def _(block=block, mask=mask):
                outs[mask][...] = results[block]
    for weight in weights:
        weight.wait()


def load_kernel(gate, down, near_gate, near_down, sems):
    copies = split_copies(gate.at[0], near_gate, sems.at[0]) + split_copies(down.at[0], near_down, sems.at[1])
    for copy in copies:
        copy.start()
    for copy in copies:
        copy.wait()


def fetch_rows(tokens, embedding, gate, down):
    vocab, features = embedding.shape
    block_rows = tokens.shape[0] // GROUP
    vmem = pl.BlockSpec(memory_space=pltpu.VMEM)
    anywhere = pl.BlockSpec(memory_space=pl.ANY)
    near = [pltpu.VMEM(gate.shape[1:], BF16), pltpu.VMEM(down.shape[1:], BF16)]
    weight_sems = pltpu.SemaphoreType.DMA((2, PARTS))
    params = pltpu.CompilerParams(vmem_limit_bytes=36 * 2**20)
    if vocab % TILE:
        segment = lax.axis_index("segment")
        local = tokens - segment * vocab
        inside = (local >= 0) & (local < vocab)
        picked = jnp.take(embedding, jnp.clip(local, 0, vocab - 1), axis=0)
        picked = jnp.where(inside[:, None], picked, jnp.zeros_like(picked))
        picked = picked.reshape(GROUP, block_rows, features)
        home = segment % GROUP
        blocks = [lax.dynamic_index_in_dim(picked, home ^ m, 0, False) for m in range(GROUP)]
        near = pl.pallas_call(
            load_kernel,
            out_shape=near,
            in_specs=[anywhere] * 2,
            out_specs=[vmem] * 2,
            scratch_shapes=[weight_sems],
            compiler_params=params,
            name="load_weights",
        )(gate, down)
        return blocks, *near
    *blocks, near_gate, near_down = pl.pallas_call(
        functools.partial(fetch_kernel, block_rows, vocab),
        out_shape=[jax.ShapeDtypeStruct((block_rows, features), BF16)] * GROUP + near,
        in_specs=[pl.BlockSpec(memory_space=pltpu.SMEM), vmem] + [anywhere] * 3,
        out_specs=[vmem] * (GROUP + 2),
        scratch_shapes=[
            pltpu.VMEM((tokens.shape[0] * TILE, features), BF16),
            pltpu.SemaphoreType.DMA((tokens.shape[0],)),
            weight_sems,
        ],
        compiler_params=params,
        name="fetch_rows",
    )(tokens, tokens.reshape(1, -1), embedding, gate, down)
    return blocks, near_gate, near_down


def position(chips):
    place = lax.axis_index("tensor")
    segment = lax.axis_index("segment")
    core = lax.rem(place, 2)
    chip = place // 2

    def share(side, turn):
        return jnp.bitwise_xor(chip, turn) * 2 + jnp.bitwise_xor(core, side)

    return segment, place, core, share


def first_kernel(chips, *refs):
    pieces, refs = refs[: 2 * GROUP], refs[2 * GROUP :]
    gain, gate, down, partial, embedded, total, norms = refs
    tokens, width = embedded.shape
    segment, place, core, share = position(chips)
    features = width // (2 * chips)
    rows = tokens // GROUP
    home = lax.rem(segment, GROUP)
    chunks = width // CHUNK
    for side in range(2):
        for turn in range(chips):
            column = pl.multiple_of(share(side, turn) * features, features)
            for block in range(GROUP):
                row = pl.multiple_of(jnp.bitwise_xor(home, block) * rows, rows)
                embedded[pl.ds(row, rows), pl.ds(column, features)] = pieces[side * GROUP + block][turn]
    gain_row = gain[pl.ds(segment // 2, 1), :]
    squares = jnp.zeros((tokens, 1), F32)
    for k in range(chunks):
        span = slice(k * CHUNK, (k + 1) * CHUNK)
        wide = embedded[:, span].astype(F32)
        squares = squares + jnp.sum(wide * wide, axis=1, keepdims=True)
        scaled = (wide * gain_row[:, span]).astype(BF16)
        product = jnp.dot(scaled, gate[span, :], preferred_element_type=F32)
        total[...] = product if k == 0 else total[...] + product
    norms[...] = squares

    @pl.when(segment < 2)
    def _():
        inverse_norm = lax.rsqrt(squares / width + EPSILON)
        activation = jax.nn.silu(total[...] * inverse_norm).astype(BF16)
        for k in range(chunks):
            span = slice(k * CHUNK, (k + 1) * CHUNK)
            product = jnp.dot(activation, down[:, span], preferred_element_type=F32)
            partial[:, span] = product.astype(BF16)


def halves(projected, core, own, send):
    half = projected.shape[0] // 2
    own[...] = projected[pl.ds(pl.multiple_of(core * half, half), half), :].astype(BF16)
    send[...] = projected[pl.ds(pl.multiple_of((1 - core) * half, half), half), :].astype(BF16)


def project_kernel(chips, *refs):
    shares, refs = refs[: 2 * GROUP + 2], refs[2 * GROUP + 2 :]
    partial, embedded, own, send, bases, seen, high, low, projected, square = refs
    width, rank = bases.shape
    segment, place, core, share = position(chips)
    features = width // (2 * chips)
    part = features // GROUP
    home = lax.rem(segment, GROUP)
    chunks = width // CHUNK
    for side in range(2):
        for turn in range(chips):
            for block in range(GROUP):
                row = share(side, turn) * features + jnp.bitwise_xor(home, block) * part
                piece, index = side * (GROUP + 1) + block, turn
                if block == GROUP - 1 and turn >= chips // 2:
                    piece, index = piece + 1, turn - chips // 2
                bases[pl.ds(pl.multiple_of(row, part), part), :] = shares[piece][index]

    @pl.when(segment < 2)
    def _():
        for k in range(chunks):
            span = slice(k * CHUNK, (k + 1) * CHUNK)
            product = jnp.dot(partial[:, span], bases[span, :], preferred_element_type=F32)
            projected[...] = product if k == 0 else projected[...] + product
        halves(projected, core, own, send)

    @pl.when(segment >= 2)
    def _():
        for k in range(chunks):
            span = slice(k * CHUNK, (k + 1) * CHUNK)
            table = bases[span, :]
            turned = table.astype(F32).T.astype(BF16)
            products = jnp.dot(turned, table, preferred_element_type=F32)
            product = jnp.dot(embedded[:, span], table, preferred_element_type=F32)
            square[...] = products if k == 0 else square[...] + products
            seen[...] = product if k == 0 else seen[...] + product
        coarse = square[...].astype(BF16)
        high[...] = coarse
        low[...] = (square[...] - coarse.astype(F32)).astype(BF16)


def enter_kernel(chips, after, bases, gain, gate, through, into, into_sum):
    segment, place, core, share = position(chips)
    through[...] = after[...]

    @pl.when(segment >= 2)
    def _():
        gain_row = gain[pl.ds(segment // 2, 1), :]
        for k in range(bases.shape[0] // CHUNK):
            span = slice(k * CHUNK, (k + 1) * CHUNK)
            turned = (bases[span, :].astype(F32).T * gain_row[:, span]).astype(BF16)
            product = jnp.dot(turned, gate[span, :], preferred_element_type=F32)
            into_sum[...] = product if k == 0 else into_sum[...] + product
        into[...] = into_sum[...].astype(BF16)


def leave_kernel(chips, after, bases, down, through, out, out_sum):
    segment, place, core, share = position(chips)
    through[...] = after[...]

    @pl.when(segment >= 2)
    def _():
        for k in range(bases.shape[0] // CHUNK):
            span = slice(k * CHUNK, (k + 1) * CHUNK)
            product = jnp.dot(down[:, span], bases[span, :], preferred_element_type=F32)
            out_sum[...] = product if k == 0 else out_sum[...] + product
        out[...] = out_sum[...].astype(BF16)


def sum_kernel(chips, *refs):
    *terms, total = refs
    total[...] = tree_sum([term[...].astype(F32) for term in terms]).astype(BF16)


def hand_kernel(step, chips, half_sum, partner, straight, crossed, result):
    @pl.when(lax.axis_index("segment") // 2 <= step)
    def _():
        result[...] = (half_sum[...].astype(F32) + partner[...].astype(F32)).astype(BF16)

    @pl.when(lax.axis_index("segment") // 2 > step)
    def _():
        result[...] = (straight[...].astype(F32) + crossed[...].astype(F32)).astype(BF16)


def collect_kernel(chips, *refs):
    *pairs, collected = refs
    half = collected.shape[1] // 2
    segment, place, core, share = position(chips)
    for section in range(len(pairs) // 2):

        @pl.when(segment // 2 == section)
        def _(section=section):
            collected[0, pl.ds(pl.multiple_of(core * half, half), half), :] = pairs[2 * section][...]
            collected[0, pl.ds(pl.multiple_of((1 - core) * half, half), half), :] = pairs[2 * section + 1][...]


def next_kernel(width, chips, *refs):
    half_own, half_other, total, norms, seen, high, low, into, out, own, send, projected = refs
    segment, place, core, share = position(chips)
    upper = jnp.where(core == 0, half_own[...], half_other[...])
    lower = jnp.where(core == 0, half_other[...], half_own[...])
    received = jnp.concatenate([upper, lower], axis=0)
    rebuilt = jnp.dot(received, high[...], preferred_element_type=F32) + jnp.dot(
        received, low[...], preferred_element_type=F32
    )
    cross = received.astype(F32) * (2.0 * seen[...] + rebuilt)
    squares = norms[...] + jnp.sum(cross, axis=1, keepdims=True)
    inverse_norm = lax.rsqrt(jnp.maximum(squares, 0.0) / width + EPSILON)
    gated = total[...] + jnp.dot(received, into[...], preferred_element_type=F32)
    activation = jax.nn.silu(gated * inverse_norm).astype(BF16)
    product = jnp.dot(activation, out[...], preferred_element_type=F32)
    alone = (lax.rem(segment, 2) == 0) & (place == 0)
    projected[...] = product + jnp.where(alone, rebuilt, jnp.zeros_like(rebuilt))
    halves(projected, core, own, send)


def kernel_call(kernel, name, inputs, outs, scratch, flops, vmem_limit=14):
    vmem = pl.BlockSpec(memory_space=pltpu.VMEM)
    return pl.pallas_call(
        functools.partial(kernel, lax.axis_size("tensor") // 2),
        out_shape=outs,
        in_specs=[vmem] * len(inputs),
        out_specs=[vmem] * len(outs),
        scratch_shapes=scratch,
        compiler_params=pltpu.CompilerParams(vmem_limit_bytes=vmem_limit * 2**20),
        cost_estimate=pl.CostEstimate(flops=flops, bytes_accessed=0, transcendentals=0),
        name=name,
    )(*inputs)


def add(terms):
    (total,) = kernel_call(sum_kernel, "add", terms, [jax.ShapeDtypeStruct(terms[0].shape, BF16)], [], 0, 2)
    return total


def per_device(tokens, embedding, gain, gate_weight, down_weight, basis):
    segments = lax.axis_size("segment")
    chips = lax.axis_size("tensor") // 2
    sections = segments // 2
    count = tokens.shape[0]
    rank = basis.shape[1]
    width, hidden = gate_weight.shape[1:]

    home = lax.axis_index("segment") % GROUP
    part = basis.shape[0] // GROUP
    quarter = lax.dynamic_slice_in_dim(basis, home * part, part, 0)
    bands = [quarter] + [swap(quarter, "tensor", 2 * m) for m in range(1, chips)]
    blocks, gate, down = fetch_rows(tokens, embedding, gate_weight, down_weight)
    blocks, bands = lax.optimization_barrier((blocks, bands))
    bands = jnp.stack(bands)
    mask = GROUP
    while mask < segments:
        blocks = [block + swap(block, "segment", mask) for block in blocks]
        mask *= 2
    complete = tree_sum(
        [block if m == 0 else swap(block, "segment", m) for m, block in enumerate(blocks)]
    )
    complete, bands = lax.optimization_barrier((complete, bands))
    shares = [bands] + [swap(bands, "segment", m) for m in range(1, GROUP - 1)]
    along = jnp.stack([complete] + [swap(complete, "tensor", 2 * m) for m in range(1, chips)])
    along, shares = lax.optimization_barrier((along, shares))
    mine = [along] + [swap(along, "segment", m) for m in range(1, GROUP)]
    mine[GROUP - 1], shares = lax.optimization_barrier((mine[GROUP - 1], shares))
    shares += [swap(shares[1][: chips // 2], "segment", 2), swap(shares[2][chips // 2 :], "segment", 1)]
    theirs = [swap(piece, "tensor", 1) for piece in mine]
    work = 2 * count * width
    partial, embedded, total, norms = kernel_call(
        first_kernel,
        "section_first",
        mine + theirs + [gain, gate, down],
        [
            pltpu.VMEM((count, width), BF16),
            pltpu.VMEM((count, width), BF16),
            pltpu.VMEM((count, hidden), F32),
            pltpu.VMEM((count, 1), F32),
        ],
        [],
        2 * work * hidden,
    )
    partial, shares[GROUP - 1], shares[GROUP] = lax.optimization_barrier(
        (partial, shares[GROUP - 1], shares[GROUP])
    )
    shares = shares + [swap(piece, "tensor", 1) for piece in shares]
    half_shape = jax.ShapeDtypeStruct((count // 2, rank), BF16)
    own, send, bases, *products = kernel_call(
        project_kernel,
        "project_first",
        shares + [partial, embedded],
        [
            half_shape,
            half_shape,
            pltpu.VMEM((width, rank), BF16),
            pltpu.VMEM((count, rank), F32),
            pltpu.VMEM((rank, rank), BF16),
            pltpu.VMEM((rank, rank), BF16),
        ],
        [pltpu.VMEM((count, rank), F32), pltpu.VMEM((rank, rank), F32)],
        work * rank,
    )

    kept = []
    for step in range(sections):
        if step > 0:
            own, send = kernel_call(
                functools.partial(next_kernel, width),
                "section_next",
                [*received, total, norms, *products],
                [half_shape, half_shape],
                [pltpu.VMEM((count, rank), F32)],
                4 * count * rank * (hidden + rank),
            )
        chip_sum = add([own, swap(send, "tensor", 1)])
        terms = [chip_sum] + [swap(chip_sum, "tensor", 2 * m) for m in range(1, chips)]
        if step == 0:
            terms[0], into = kernel_call(
                enter_kernel,
                "enter",
                [chip_sum, bases, gain, gate],
                [half_shape, pltpu.VMEM((rank, hidden), BF16)],
                [pltpu.VMEM((rank, hidden), F32)],
                2 * hidden * width * rank,
            )
        half_sum = add(terms)
        partner = swap(half_sum, "segment", 1)
        if step + 1 < sections:
            straight, crossed = onward(half_sum, 0), onward(half_sum, 1)
            if step == 0:
                half_sum, out = kernel_call(
                    leave_kernel,
                    "leave",
                    [half_sum, bases, down],
                    [half_shape, pltpu.VMEM((hidden, rank), BF16)],
                    [pltpu.VMEM((hidden, rank), F32)],
                    2 * hidden * width * rank,
                )
                products += [into, out]
            (result,) = kernel_call(
                functools.partial(hand_kernel, step),
                "hand",
                [half_sum, partner, straight, crossed],
                [half_shape],
                [],
                0,
                2,
            )
        else:
            result = add([half_sum, partner])
        received = (result, swap(result, "tensor", 1))
        kept += received
    (collected,) = kernel_call(
        collect_kernel, "collect", kept, [jax.ShapeDtypeStruct((1, count, rank), BF16)], [], 0, 2
    )
    return collected


def solution(mesh):
    placed = (
        P(),
        P("segment", "tensor"),
        P(),
        P("segment", None, "tensor"),
        P("segment", "tensor", None),
        P("tensor", None),
    )
    return jax.shard_map(
        per_device, mesh=mesh, in_specs=placed, out_specs=P("segment", None, None), check_vma=False
    )
```

```python
import functools

import jax
import jax.numpy as jnp
from jax import lax
from jax.experimental import pallas as pl
from jax.experimental.pallas import tpu as pltpu
from jax.sharding import PartitionSpec as P

EPSILON = 1e-05
GROUP = 4
TILE = 16
PARTS = 8
CHUNK = 512
F32 = jnp.float32
BF16 = jnp.bfloat16


def swap(value, axis, mask):
    return lax.ppermute(value, axis, [(i, i ^ mask) for i in range(lax.axis_size(axis))])


def onward(value, flip):
    size = lax.axis_size("segment")
    return lax.ppermute(value, "segment", [(i, (i ^ flip) + 2) for i in range(size - 2)])


def tree_sum(values):
    while len(values) > 1:
        values = [values[i] + values[i + 1] for i in range(0, len(values), 2)]
    return values[0]


def split_copies(source, target, sems):
    rows = source.shape[0]
    parts = max(p for p in range(1, PARTS + 1) if rows % (TILE * p) == 0)
    size = rows // parts
    return [
        pltpu.make_async_copy(
            source.at[pl.ds(k * size, size), :], target.at[pl.ds(k * size, size), :], sems.at[k]
        )
        for k in range(parts)
    ]


def fetch_kernel(block_rows, vocab, tokens_smem, tokens_row, table, gate, down, *refs):
    outs, (near_gate, near_down, buffer, sems, weight_sems) = refs[:GROUP], refs[GROUP:]
    weights = split_copies(gate.at[0], near_gate, weight_sems.at[0])
    weights += split_copies(down.at[0], near_down, weight_sems.at[1])
    segment = lax.axis_index("segment")
    low = segment * vocab
    count = GROUP * block_rows

    def held(i):
        local = tokens_smem[i] - low
        return local, (local >= 0) & (local < vocab)

    def copy(i, local):
        first = pl.multiple_of((local // TILE) * TILE, TILE)
        place = pl.multiple_of(i * TILE, TILE)
        return pltpu.make_async_copy(
            table.at[pl.ds(first, TILE), :], buffer.at[pl.ds(place, TILE), :], sems.at[i]
        )

    def start(i, carry):
        local, here = held(i)

        @pl.when(here)
        def _():
            copy(i, local).start()

        return carry

    def finish(i, carry):
        local, here = held(i)

        @pl.when(here)
        def _():
            copy(i, local).wait()

        return carry

    buffer[...] = jnp.zeros_like(buffer)
    for weight in weights:
        weight.start()
    lax.fori_loop(0, count, start, 0, unroll=8)
    wanted = tokens_row[...] - low
    inside = (wanted >= 0) & (wanted < vocab)
    code = jnp.where(inside, lax.rem(wanted, TILE), TILE)
    rows = lax.broadcasted_iota(jnp.int32, (count, count), 0)
    columns = lax.broadcasted_iota(jnp.int32, (count, count), 1)
    code_column = jnp.sum(jnp.where(rows == columns, code, 0), axis=1, keepdims=True)
    lax.fori_loop(0, count, finish, 0, unroll=8)
    home = lax.rem(segment, GROUP)
    wide = block_rows * TILE
    row_of = lax.broadcasted_iota(jnp.int32, (block_rows, wide), 0)
    lane_of = lax.broadcasted_iota(jnp.int32, (block_rows, wide), 1)
    results = []
    for block in range(GROUP):
        code_block = code_column[block * block_rows : (block + 1) * block_rows]
        hot = (lane_of == row_of * TILE + code_block) & (code_block < TILE)
        hot = jnp.where(hot, 1.0, 0.0).astype(BF16)
        results.append(
            jnp.dot(
                hot, buffer[block * wide : (block + 1) * wide, :], preferred_element_type=F32
            ).astype(BF16)
        )
    for block in range(GROUP):
        for mask in range(GROUP):

            @pl.when(jnp.bitwise_xor(home, mask) == block)
            def _(block=block, mask=mask):
                outs[mask][...] = results[block]
    for weight in weights:
        weight.wait()


def load_kernel(gate, down, near_gate, near_down, sems):
    copies = split_copies(gate.at[0], near_gate, sems.at[0]) + split_copies(down.at[0], near_down, sems.at[1])
    for copy in copies:
        copy.start()
    for copy in copies:
        copy.wait()


def fetch_rows(tokens, embedding, gate, down):
    vocab, features = embedding.shape
    block_rows = tokens.shape[0] // GROUP
    vmem = pl.BlockSpec(memory_space=pltpu.VMEM)
    anywhere = pl.BlockSpec(memory_space=pl.ANY)
    near = [pltpu.VMEM(gate.shape[1:], BF16), pltpu.VMEM(down.shape[1:], BF16)]
    weight_sems = pltpu.SemaphoreType.DMA((2, PARTS))
    params = pltpu.CompilerParams(vmem_limit_bytes=36 * 2**20)
    if vocab % TILE:
        segment = lax.axis_index("segment")
        local = tokens - segment * vocab
        inside = (local >= 0) & (local < vocab)
        picked = jnp.take(embedding, jnp.clip(local, 0, vocab - 1), axis=0)
        picked = jnp.where(inside[:, None], picked, jnp.zeros_like(picked))
        picked = picked.reshape(GROUP, block_rows, features)
        home = segment % GROUP
        blocks = [lax.dynamic_index_in_dim(picked, home ^ m, 0, False) for m in range(GROUP)]
        near = pl.pallas_call(
            load_kernel,
            out_shape=near,
            in_specs=[anywhere] * 2,
            out_specs=[vmem] * 2,
            scratch_shapes=[weight_sems],
            compiler_params=params,
            name="load_weights",
        )(gate, down)
        return blocks, *near
    *blocks, near_gate, near_down = pl.pallas_call(
        functools.partial(fetch_kernel, block_rows, vocab),
        out_shape=[jax.ShapeDtypeStruct((block_rows, features), BF16)] * GROUP + near,
        in_specs=[pl.BlockSpec(memory_space=pltpu.SMEM), vmem] + [anywhere] * 3,
        out_specs=[vmem] * (GROUP + 2),
        scratch_shapes=[
            pltpu.VMEM((tokens.shape[0] * TILE, features), BF16),
            pltpu.SemaphoreType.DMA((tokens.shape[0],)),
            weight_sems,
        ],
        compiler_params=params,
        name="fetch_rows",
    )(tokens, tokens.reshape(1, -1), embedding, gate, down)
    return blocks, near_gate, near_down


def position(chips):
    place = lax.axis_index("tensor")
    segment = lax.axis_index("segment")
    core = lax.rem(place, 2)
    chip = place // 2

    def share(side, turn):
        return jnp.bitwise_xor(chip, turn) * 2 + jnp.bitwise_xor(core, side)

    return segment, place, core, share


def first_kernel(chips, *refs):
    pieces, refs = refs[: 2 * GROUP], refs[2 * GROUP :]
    gain, gate, down, partial, embedded, total, norms = refs
    tokens, width = embedded.shape
    segment, place, core, share = position(chips)
    features = width // (2 * chips)
    rows = tokens // GROUP
    home = lax.rem(segment, GROUP)
    chunks = width // CHUNK
    for side in range(2):
        for turn in range(chips):
            column = pl.multiple_of(share(side, turn) * features, features)
            for block in range(GROUP):
                row = pl.multiple_of(jnp.bitwise_xor(home, block) * rows, rows)
                embedded[pl.ds(row, rows), pl.ds(column, features)] = pieces[side * GROUP + block][turn]
    gain_row = gain[pl.ds(segment // 2, 1), :]
    squares = jnp.zeros((tokens, 1), F32)
    for k in range(chunks):
        span = slice(k * CHUNK, (k + 1) * CHUNK)
        wide = embedded[:, span].astype(F32)
        squares = squares + jnp.sum(wide * wide, axis=1, keepdims=True)
        scaled = (wide * gain_row[:, span]).astype(BF16)
        product = jnp.dot(scaled, gate[span, :], preferred_element_type=F32)
        total[...] = product if k == 0 else total[...] + product
    norms[...] = squares

    @pl.when(segment < 2)
    def _():
        inverse_norm = lax.rsqrt(squares / width + EPSILON)
        activation = jax.nn.silu(total[...] * inverse_norm).astype(BF16)
        for k in range(chunks):
            span = slice(k * CHUNK, (k + 1) * CHUNK)
            product = jnp.dot(activation, down[:, span], preferred_element_type=F32)
            partial[:, span] = product.astype(BF16)


def halves(projected, core, own, send):
    half = projected.shape[0] // 2
    own[...] = projected[pl.ds(pl.multiple_of(core * half, half), half), :].astype(BF16)
    send[...] = projected[pl.ds(pl.multiple_of((1 - core) * half, half), half), :].astype(BF16)


def project_kernel(chips, *refs):
    shares, refs = refs[: 2 * GROUP + 2], refs[2 * GROUP + 2 :]
    partial, own, send, bases, projected = refs
    width, rank = bases.shape
    segment, place, core, share = position(chips)
    features = width // (2 * chips)
    part = features // GROUP
    home = lax.rem(segment, GROUP)
    chunks = width // CHUNK
    for side in range(2):
        for turn in range(chips):
            for block in range(GROUP):
                row = share(side, turn) * features + jnp.bitwise_xor(home, block) * part
                piece, index = side * (GROUP + 1) + block, turn
                if block == GROUP - 1 and turn >= chips // 2:
                    piece, index = piece + 1, turn - chips // 2
                bases[pl.ds(pl.multiple_of(row, part), part), :] = shares[piece][index]

    @pl.when(segment < 2)
    def _():
        for k in range(chunks):
            span = slice(k * CHUNK, (k + 1) * CHUNK)
            product = jnp.dot(partial[:, span], bases[span, :], preferred_element_type=F32)
            projected[...] = product if k == 0 else projected[...] + product
        halves(projected, core, own, send)


def enter_kernel(chips, *refs):
    after, bases, gain, gate, embedded, through, seen, high, low, into, into_sum, square = refs
    segment, place, core, share = position(chips)
    through[...] = after[...]

    @pl.when(segment >= 2)
    def _():
        gain_row = gain[pl.ds(segment // 2, 1), :]
        for k in range(bases.shape[0] // CHUNK):
            span = slice(k * CHUNK, (k + 1) * CHUNK)
            table = bases[span, :]
            turned = table.astype(F32).T
            scaled = (turned * gain_row[:, span]).astype(BF16)
            products = [
                jnp.dot(scaled, gate[span, :], preferred_element_type=F32),
                jnp.dot(turned.astype(BF16), table, preferred_element_type=F32),
                jnp.dot(embedded[:, span], table, preferred_element_type=F32),
            ]
            for target, product in zip((into_sum, square, seen), products):
                target[...] = product if k == 0 else target[...] + product
        into[...] = into_sum[...].astype(BF16)
        coarse = square[...].astype(BF16)
        high[...] = coarse
        low[...] = (square[...] - coarse.astype(F32)).astype(BF16)


def leave_kernel(chips, after, bases, down, through, out, out_sum):
    segment, place, core, share = position(chips)
    through[...] = after[...]

    @pl.when(segment >= 2)
    def _():
        for k in range(bases.shape[0] // CHUNK):
            span = slice(k * CHUNK, (k + 1) * CHUNK)
            product = jnp.dot(down[:, span], bases[span, :], preferred_element_type=F32)
            out_sum[...] = product if k == 0 else out_sum[...] + product
        out[...] = out_sum[...].astype(BF16)


def sum_kernel(chips, *refs):
    *terms, total = refs
    total[...] = tree_sum([term[...].astype(F32) for term in terms]).astype(BF16)


def choose_kernel(step, chips, half_sum, *refs):
    *terms, chosen = refs

    @pl.when(lax.axis_index("segment") // 2 < step)
    def _():
        chosen[...] = half_sum[...]

    @pl.when(lax.axis_index("segment") // 2 >= step)
    def _():
        chosen[...] = tree_sum([term[...].astype(F32) for term in terms]).astype(BF16)


def collect_kernel(chips, near, far, collected):
    half = collected.shape[1] // 2
    segment, place, core, share = position(chips)
    collected[0, pl.ds(pl.multiple_of(core * half, half), half), :] = near[...]
    collected[0, pl.ds(pl.multiple_of((1 - core) * half, half), half), :] = far[...]


def next_kernel(width, chips, *refs):
    half_own, half_other, total, norms, seen, high, low, into, out, own, send, projected = refs
    segment, place, core, share = position(chips)
    upper = jnp.where(core == 0, half_own[...], half_other[...])
    lower = jnp.where(core == 0, half_other[...], half_own[...])
    received = jnp.concatenate([upper, lower], axis=0)
    rebuilt = jnp.dot(received, high[...], preferred_element_type=F32) + jnp.dot(
        received, low[...], preferred_element_type=F32
    )
    cross = received.astype(F32) * (2.0 * seen[...] + rebuilt)
    squares = norms[...] + jnp.sum(cross, axis=1, keepdims=True)
    inverse_norm = lax.rsqrt(jnp.maximum(squares, 0.0) / width + EPSILON)
    gated = total[...] + jnp.dot(received, into[...], preferred_element_type=F32)
    activation = jax.nn.silu(gated * inverse_norm).astype(BF16)
    product = jnp.dot(activation, out[...], preferred_element_type=F32)
    alone = (lax.rem(segment, 2) == 0) & (place == 0)
    projected[...] = product + jnp.where(alone, rebuilt, jnp.zeros_like(rebuilt))
    halves(projected, core, own, send)


def kernel_call(kernel, name, inputs, outs, scratch, flops, vmem_limit=14):
    vmem = pl.BlockSpec(memory_space=pltpu.VMEM)
    return pl.pallas_call(
        functools.partial(kernel, lax.axis_size("tensor") // 2),
        out_shape=outs,
        in_specs=[vmem] * len(inputs),
        out_specs=[vmem] * len(outs),
        scratch_shapes=scratch,
        compiler_params=pltpu.CompilerParams(vmem_limit_bytes=vmem_limit * 2**20),
        cost_estimate=pl.CostEstimate(flops=flops, bytes_accessed=0, transcendentals=0),
        name=name,
    )(*inputs)


def choose(step, half_sum, terms):
    (chosen,) = kernel_call(
        functools.partial(choose_kernel, step),
        "choose",
        [half_sum, *terms],
        [jax.ShapeDtypeStruct(half_sum.shape, BF16)],
        [],
        0,
        2,
    )
    return chosen


def add(terms):
    (total,) = kernel_call(sum_kernel, "add", terms, [jax.ShapeDtypeStruct(terms[0].shape, BF16)], [], 0, 2)
    return total


def per_device(tokens, embedding, gain, gate_weight, down_weight, basis):
    segments = lax.axis_size("segment")
    chips = lax.axis_size("tensor") // 2
    sections = segments // 2
    count = tokens.shape[0]
    rank = basis.shape[1]
    width, hidden = gate_weight.shape[1:]

    home = lax.axis_index("segment") % GROUP
    part = basis.shape[0] // GROUP
    quarter = lax.dynamic_slice_in_dim(basis, home * part, part, 0)
    bands = [quarter] + [swap(quarter, "tensor", 2 * m) for m in range(1, chips)]
    blocks, gate, down = fetch_rows(tokens, embedding, gate_weight, down_weight)
    blocks, bands = lax.optimization_barrier((blocks, bands))
    bands = jnp.stack(bands)
    mask = GROUP
    while mask < segments:
        blocks = [block + swap(block, "segment", mask) for block in blocks]
        mask *= 2
    arrived = [blocks[0]] + [swap(blocks[m], "segment", m) for m in range(1, GROUP)]
    arrived[1], bands = lax.optimization_barrier((arrived[1], bands))
    complete = tree_sum(arrived)
    shares = [bands] + [swap(bands, "segment", m) for m in range(1, GROUP - 1)]
    along = jnp.stack([complete] + [swap(complete, "tensor", 2 * m) for m in range(1, chips)])
    mine = [along] + [swap(along, "segment", m) for m in range(1, GROUP)]
    mine[GROUP - 1], shares = lax.optimization_barrier((mine[GROUP - 1], shares))
    shares += [swap(shares[1][: chips // 2], "segment", 2), swap(shares[2][chips // 2 :], "segment", 1)]
    theirs = [swap(piece, "tensor", 1) for piece in mine]
    work = 2 * count * width
    partial, embedded, total, norms = kernel_call(
        first_kernel,
        "section_first",
        mine + theirs + [gain, gate, down],
        [
            pltpu.VMEM((count, width), BF16),
            pltpu.VMEM((count, width), BF16),
            pltpu.VMEM((count, hidden), F32),
            pltpu.VMEM((count, 1), F32),
        ],
        [],
        2 * work * hidden,
    )
    partial, shares[GROUP - 1], shares[GROUP] = lax.optimization_barrier(
        (partial, shares[GROUP - 1], shares[GROUP])
    )
    shares = shares + [swap(piece, "tensor", 1) for piece in shares]
    half_shape = jax.ShapeDtypeStruct((count // 2, rank), BF16)
    own, send, bases = kernel_call(
        project_kernel,
        "project_first",
        shares + [partial],
        [half_shape, half_shape, pltpu.VMEM((width, rank), BF16)],
        [pltpu.VMEM((count, rank), F32)],
        work * rank,
    )

    received = half_sum = None
    for step in range(sections):
        if step > 0:
            own, send = kernel_call(
                functools.partial(next_kernel, width),
                "section_next",
                [*received, total, norms, *products],
                [half_shape, half_shape],
                [pltpu.VMEM((count, rank), F32)],
                4 * count * rank * (hidden + rank),
            )
        chip_sum = add([own, swap(send, "tensor", 1)])
        terms = [chip_sum] + [swap(chip_sum, "tensor", 2 * m) for m in range(1, chips)]
        if step == 0:
            terms[0], *products = kernel_call(
                enter_kernel,
                "enter",
                [chip_sum, bases, gain, gate, embedded],
                [
                    half_shape,
                    pltpu.VMEM((count, rank), F32),
                    pltpu.VMEM((rank, rank), BF16),
                    pltpu.VMEM((rank, rank), BF16),
                    pltpu.VMEM((rank, hidden), BF16),
                ],
                [pltpu.VMEM((rank, hidden), F32), pltpu.VMEM((rank, rank), F32)],
                2 * rank * width * (hidden + rank + count),
            )
        half_sum = add(terms) if step == 0 else choose(step, half_sum, terms)
        if step + 1 < sections:
            straight, crossed = onward(half_sum, 0), onward(half_sum, 1)
            if step == 0:
                half_sum, out = kernel_call(
                    leave_kernel,
                    "leave",
                    [half_sum, bases, down],
                    [half_shape, pltpu.VMEM((hidden, rank), BF16)],
                    [pltpu.VMEM((hidden, rank), F32)],
                    2 * hidden * width * rank,
                )
                products += [out]
                straight, half_sum = lax.optimization_barrier((straight, half_sum))
            handed = add([straight, crossed])
            received = [handed, swap(handed, "tensor", 1)]
    result = add([half_sum, swap(half_sum, "segment", 1)])
    (collected,) = kernel_call(
        collect_kernel,
        "collect",
        [result, swap(result, "tensor", 1)],
        [jax.ShapeDtypeStruct((1, count, rank), BF16)],
        [],
        0,
        2,
    )
    return collected


def solution(mesh):
    placed = (
        P(),
        P("segment", "tensor"),
        P(),
        P("segment", None, "tensor"),
        P("segment", "tensor", None),
        P("tensor", None),
    )
    return jax.shard_map(
        per_device, mesh=mesh, in_specs=placed, out_specs=P("segment", None, None), check_vma=False
    )
```

```python
import functools

import jax
import jax.numpy as jnp
from jax import lax
from jax.experimental import pallas as pl
from jax.experimental.pallas import tpu as pltpu
from jax.sharding import PartitionSpec as P

EPSILON = 1e-05
GROUP = 4
TILE = 16
PARTS = 8
CHUNK = 512
F32 = jnp.float32
BF16 = jnp.bfloat16


def swap(value, axis, mask):
    return lax.ppermute(value, axis, [(i, i ^ mask) for i in range(lax.axis_size(axis))])


def onward(value, flip):
    size = lax.axis_size("segment")
    return lax.ppermute(value, "segment", [(i, (i ^ flip) + 2) for i in range(size - 2)])


def tree_sum(values):
    while len(values) > 1:
        values = [values[i] + values[i + 1] for i in range(0, len(values), 2)]
    return values[0]


def split_copies(source, target, sems):
    rows = source.shape[0]
    parts = max(p for p in range(1, PARTS + 1) if rows % (TILE * p) == 0)
    size = rows // parts
    return [
        pltpu.make_async_copy(
            source.at[pl.ds(k * size, size), :], target.at[pl.ds(k * size, size), :], sems.at[k]
        )
        for k in range(parts)
    ]


def fetch_kernel(block_rows, vocab, tokens_smem, tokens_row, table, gate, down, *refs):
    outs, (near_gate, near_down, buffer, sems, weight_sems) = refs[:GROUP], refs[GROUP:]
    weights = split_copies(gate.at[0], near_gate, weight_sems.at[0])
    weights += split_copies(down.at[0], near_down, weight_sems.at[1])
    segment = lax.axis_index("segment")
    low = segment * vocab
    count = GROUP * block_rows

    def held(i):
        local = tokens_smem[i] - low
        return local, (local >= 0) & (local < vocab)

    def copy(i, local):
        first = pl.multiple_of((local // TILE) * TILE, TILE)
        place = pl.multiple_of(i * TILE, TILE)
        return pltpu.make_async_copy(
            table.at[pl.ds(first, TILE), :], buffer.at[pl.ds(place, TILE), :], sems.at[i]
        )

    def start(i, carry):
        local, here = held(i)

        @pl.when(here)
        def _():
            copy(i, local).start()

        return carry

    def finish(i, carry):
        local, here = held(i)

        @pl.when(here)
        def _():
            copy(i, local).wait()

        return carry

    buffer[...] = jnp.zeros_like(buffer)
    for weight in weights:
        weight.start()
    lax.fori_loop(0, count, start, 0, unroll=8)
    wanted = tokens_row[...] - low
    inside = (wanted >= 0) & (wanted < vocab)
    code = jnp.where(inside, lax.rem(wanted, TILE), TILE)
    rows = lax.broadcasted_iota(jnp.int32, (count, count), 0)
    columns = lax.broadcasted_iota(jnp.int32, (count, count), 1)
    code_column = jnp.sum(jnp.where(rows == columns, code, 0), axis=1, keepdims=True)
    lax.fori_loop(0, count, finish, 0, unroll=8)
    home = lax.rem(segment, GROUP)
    wide = block_rows * TILE
    row_of = lax.broadcasted_iota(jnp.int32, (block_rows, wide), 0)
    lane_of = lax.broadcasted_iota(jnp.int32, (block_rows, wide), 1)
    results = []
    for block in range(GROUP):
        code_block = code_column[block * block_rows : (block + 1) * block_rows]
        hot = (lane_of == row_of * TILE + code_block) & (code_block < TILE)
        hot = jnp.where(hot, 1.0, 0.0).astype(BF16)
        results.append(
            jnp.dot(
                hot, buffer[block * wide : (block + 1) * wide, :], preferred_element_type=F32
            ).astype(BF16)
        )
    for block in range(GROUP):
        for mask in range(GROUP):

            @pl.when(jnp.bitwise_xor(home, mask) == block)
            def _(block=block, mask=mask):
                outs[mask][...] = results[block]
    for weight in weights:
        weight.wait()


def load_kernel(gate, down, near_gate, near_down, sems):
    copies = split_copies(gate.at[0], near_gate, sems.at[0]) + split_copies(down.at[0], near_down, sems.at[1])
    for copy in copies:
        copy.start()
    for copy in copies:
        copy.wait()


def fetch_rows(tokens, embedding, gate, down):
    vocab, features = embedding.shape
    block_rows = tokens.shape[0] // GROUP
    vmem = pl.BlockSpec(memory_space=pltpu.VMEM)
    anywhere = pl.BlockSpec(memory_space=pl.ANY)
    near = [pltpu.VMEM(gate.shape[1:], BF16), pltpu.VMEM(down.shape[1:], BF16)]
    weight_sems = pltpu.SemaphoreType.DMA((2, PARTS))
    params = pltpu.CompilerParams(vmem_limit_bytes=36 * 2**20)
    if vocab % TILE:
        segment = lax.axis_index("segment")
        local = tokens - segment * vocab
        inside = (local >= 0) & (local < vocab)
        picked = jnp.take(embedding, jnp.clip(local, 0, vocab - 1), axis=0)
        picked = jnp.where(inside[:, None], picked, jnp.zeros_like(picked))
        picked = picked.reshape(GROUP, block_rows, features)
        home = segment % GROUP
        blocks = [lax.dynamic_index_in_dim(picked, home ^ m, 0, False) for m in range(GROUP)]
        near = pl.pallas_call(
            load_kernel,
            out_shape=near,
            in_specs=[anywhere] * 2,
            out_specs=[vmem] * 2,
            scratch_shapes=[weight_sems],
            compiler_params=params,
            name="load_weights",
        )(gate, down)
        return blocks, *near
    *blocks, near_gate, near_down = pl.pallas_call(
        functools.partial(fetch_kernel, block_rows, vocab),
        out_shape=[jax.ShapeDtypeStruct((block_rows, features), BF16)] * GROUP + near,
        in_specs=[pl.BlockSpec(memory_space=pltpu.SMEM), vmem] + [anywhere] * 3,
        out_specs=[vmem] * (GROUP + 2),
        scratch_shapes=[
            pltpu.VMEM((tokens.shape[0] * TILE, features), BF16),
            pltpu.SemaphoreType.DMA((tokens.shape[0],)),
            weight_sems,
        ],
        compiler_params=params,
        name="fetch_rows",
    )(tokens, tokens.reshape(1, -1), embedding, gate, down)
    return blocks, near_gate, near_down


def position(chips):
    place = lax.axis_index("tensor")
    segment = lax.axis_index("segment")
    core = lax.rem(place, 2)
    chip = place // 2

    def share(side, turn):
        return jnp.bitwise_xor(chip, turn) * 2 + jnp.bitwise_xor(core, side)

    return segment, place, core, share


def first_kernel(chips, *refs):
    pieces, refs = refs[: 2 * GROUP], refs[2 * GROUP :]
    gain, gate, down, partial, embedded, total, norms = refs
    tokens, width = embedded.shape
    segment, place, core, share = position(chips)
    features = width // (2 * chips)
    rows = tokens // GROUP
    home = lax.rem(segment, GROUP)
    chunks = width // CHUNK
    for side in range(2):
        for turn in range(chips):
            column = pl.multiple_of(share(side, turn) * features, features)
            for block in range(GROUP):
                row = pl.multiple_of(jnp.bitwise_xor(home, block) * rows, rows)
                embedded[pl.ds(row, rows), pl.ds(column, features)] = pieces[side * GROUP + block][turn]
    gain_row = gain[pl.ds(segment // 2, 1), :]
    squares = jnp.zeros((tokens, 1), F32)
    for k in range(chunks):
        span = slice(k * CHUNK, (k + 1) * CHUNK)
        wide = embedded[:, span].astype(F32)
        squares = squares + jnp.sum(wide * wide, axis=1, keepdims=True)
        scaled = (wide * gain_row[:, span]).astype(BF16)
        product = jnp.dot(scaled, gate[span, :], preferred_element_type=F32)
        total[...] = product if k == 0 else total[...] + product
    norms[...] = squares

    @pl.when(segment < 2)
    def _():
        inverse_norm = lax.rsqrt(squares / width + EPSILON)
        activation = jax.nn.silu(total[...] * inverse_norm).astype(BF16)
        for k in range(chunks):
            span = slice(k * CHUNK, (k + 1) * CHUNK)
            product = jnp.dot(activation, down[:, span], preferred_element_type=F32)
            partial[:, span] = product.astype(BF16)


def halves(projected, core, own, send):
    half = projected.shape[0] // 2
    own[...] = projected[pl.ds(pl.multiple_of(core * half, half), half), :].astype(BF16)
    send[...] = projected[pl.ds(pl.multiple_of((1 - core) * half, half), half), :].astype(BF16)


def project_kernel(chips, *refs):
    shares, refs = refs[: 2 * GROUP + 2], refs[2 * GROUP + 2 :]
    partial, own, send, bases, projected = refs
    width, rank = bases.shape
    segment, place, core, share = position(chips)
    features = width // (2 * chips)
    part = features // GROUP
    home = lax.rem(segment, GROUP)
    chunks = width // CHUNK
    for side in range(2):
        for turn in range(chips):
            for block in range(GROUP):
                row = share(side, turn) * features + jnp.bitwise_xor(home, block) * part
                piece, index = side * (GROUP + 1) + block, turn
                if block == GROUP - 1 and turn >= chips // 2:
                    piece, index = piece + 1, turn - chips // 2
                bases[pl.ds(pl.multiple_of(row, part), part), :] = shares[piece][index]

    @pl.when(segment < 2)
    def _():
        for k in range(chunks):
            span = slice(k * CHUNK, (k + 1) * CHUNK)
            product = jnp.dot(partial[:, span], bases[span, :], preferred_element_type=F32)
            projected[...] = product if k == 0 else projected[...] + product
        halves(projected, core, own, send)


def enter_kernel(chips, *refs):
    after, bases, gain, gate, embedded, through, seen, high, low, into, into_sum, square = refs
    segment, place, core, share = position(chips)
    through[...] = after[...]

    @pl.when(segment >= 2)
    def _():
        gain_row = gain[pl.ds(segment // 2, 1), :]
        for k in range(bases.shape[0] // CHUNK):
            span = slice(k * CHUNK, (k + 1) * CHUNK)
            table = bases[span, :]
            turned = table.astype(F32).T
            scaled = (turned * gain_row[:, span]).astype(BF16)
            products = [
                jnp.dot(scaled, gate[span, :], preferred_element_type=F32),
                jnp.dot(turned.astype(BF16), table, preferred_element_type=F32),
                jnp.dot(embedded[:, span], table, preferred_element_type=F32),
            ]
            for target, product in zip((into_sum, square, seen), products):
                target[...] = product if k == 0 else target[...] + product
        into[...] = into_sum[...].astype(BF16)
        coarse = square[...].astype(BF16)
        high[...] = coarse
        low[...] = (square[...] - coarse.astype(F32)).astype(BF16)


def leave_kernel(chips, after, bases, down, through, out, out_sum):
    segment, place, core, share = position(chips)
    through[...] = after[...]

    @pl.when(segment >= 2)
    def _():
        for k in range(bases.shape[0] // CHUNK):
            span = slice(k * CHUNK, (k + 1) * CHUNK)
            product = jnp.dot(down[:, span], bases[span, :], preferred_element_type=F32)
            out_sum[...] = product if k == 0 else out_sum[...] + product
        out[...] = out_sum[...].astype(BF16)


def sum_kernel(chips, *refs):
    *terms, total = refs
    total[...] = tree_sum([term[...].astype(F32) for term in terms]).astype(BF16)


def choose_kernel(step, chips, half_sum, *refs):
    *terms, chosen = refs

    @pl.when(lax.axis_index("segment") // 2 < step)
    def _():
        chosen[...] = half_sum[...]

    @pl.when(lax.axis_index("segment") // 2 >= step)
    def _():
        chosen[...] = tree_sum([term[...].astype(F32) for term in terms]).astype(BF16)


def collect_kernel(chips, near, far, collected):
    half = collected.shape[1] // 2
    segment, place, core, share = position(chips)
    collected[0, pl.ds(pl.multiple_of(core * half, half), half), :] = near[...]
    collected[0, pl.ds(pl.multiple_of((1 - core) * half, half), half), :] = far[...]


def next_kernel(width, chips, *refs):
    half_own, half_other, total, norms, seen, high, low, into, out, own, send, projected = refs
    segment, place, core, share = position(chips)
    upper = jnp.where(core == 0, half_own[...], half_other[...])
    lower = jnp.where(core == 0, half_other[...], half_own[...])
    received = jnp.concatenate([upper, lower], axis=0)
    rebuilt = jnp.dot(received, high[...], preferred_element_type=F32) + jnp.dot(
        received, low[...], preferred_element_type=F32
    )
    cross = received.astype(F32) * (2.0 * seen[...] + rebuilt)
    squares = norms[...] + jnp.sum(cross, axis=1, keepdims=True)
    inverse_norm = lax.rsqrt(jnp.maximum(squares, 0.0) / width + EPSILON)
    gated = total[...] + jnp.dot(received, into[...], preferred_element_type=F32)
    activation = jax.nn.silu(gated * inverse_norm).astype(BF16)
    product = jnp.dot(activation, out[...], preferred_element_type=F32)
    alone = (lax.rem(segment, 2) == 0) & (place == 0)
    projected[...] = product + jnp.where(alone, rebuilt, jnp.zeros_like(rebuilt))
    halves(projected, core, own, send)


def kernel_call(kernel, name, inputs, outs, scratch, flops, vmem_limit=14):
    vmem = pl.BlockSpec(memory_space=pltpu.VMEM)
    return pl.pallas_call(
        functools.partial(kernel, lax.axis_size("tensor") // 2),
        out_shape=outs,
        in_specs=[vmem] * len(inputs),
        out_specs=[vmem] * len(outs),
        scratch_shapes=scratch,
        compiler_params=pltpu.CompilerParams(vmem_limit_bytes=vmem_limit * 2**20),
        cost_estimate=pl.CostEstimate(flops=flops, bytes_accessed=0, transcendentals=0),
        name=name,
    )(*inputs)


def choose(step, half_sum, terms):
    (chosen,) = kernel_call(
        functools.partial(choose_kernel, step),
        "choose",
        [half_sum, *terms],
        [jax.ShapeDtypeStruct(half_sum.shape, BF16)],
        [],
        0,
        2,
    )
    return chosen


def add(terms):
    (total,) = kernel_call(sum_kernel, "add", terms, [jax.ShapeDtypeStruct(terms[0].shape, BF16)], [], 0, 2)
    return total


def per_device(tokens, embedding, gain, gate_weight, down_weight, basis):
    segments = lax.axis_size("segment")
    chips = lax.axis_size("tensor") // 2
    sections = segments // 2
    count = tokens.shape[0]
    rank = basis.shape[1]
    width, hidden = gate_weight.shape[1:]

    home = lax.axis_index("segment") % GROUP
    part = basis.shape[0] // GROUP
    quarter = lax.dynamic_slice_in_dim(basis, home * part, part, 0)
    bands = [quarter] + [swap(quarter, "tensor", 2 * m) for m in range(1, chips)]
    blocks, gate, down = fetch_rows(tokens, embedding, gate_weight, down_weight)
    blocks, bands = lax.optimization_barrier((blocks, bands))
    bands = jnp.stack(bands)
    mask = GROUP
    while mask < segments:
        blocks = [block + swap(block, "segment", mask) for block in blocks]
        mask *= 2
    arrived = [blocks[0]] + [swap(blocks[m], "segment", m) for m in range(1, GROUP)]
    arrived[1], bands = lax.optimization_barrier((arrived[1], bands))
    complete = tree_sum(arrived)
    shares = [bands] + [swap(bands, "segment", m) for m in range(1, GROUP - 1)]
    along = jnp.stack([complete] + [swap(complete, "tensor", 2 * m) for m in range(1, chips)])
    mine = [along] + [swap(along, "segment", m) for m in range(1, GROUP)]
    mine[GROUP - 1], _ = lax.optimization_barrier((mine[GROUP - 1], shares))
    shares += [swap(shares[1][: chips // 2], "segment", 2), swap(shares[2][chips // 2 :], "segment", 1)]
    theirs = [swap(piece, "tensor", 1) for piece in mine]
    work = 2 * count * width
    partial, embedded, total, norms = kernel_call(
        first_kernel,
        "section_first",
        mine + theirs + [gain, gate, down],
        [
            pltpu.VMEM((count, width), BF16),
            pltpu.VMEM((count, width), BF16),
            pltpu.VMEM((count, hidden), F32),
            pltpu.VMEM((count, 1), F32),
        ],
        [],
        0,
    )
    partial, shares[GROUP - 1], shares[GROUP] = lax.optimization_barrier(
        (partial, shares[GROUP - 1], shares[GROUP])
    )
    shares = shares + [swap(piece, "tensor", 1) for piece in shares]
    half_shape = jax.ShapeDtypeStruct((count // 2, rank), BF16)
    own, send, bases = kernel_call(
        project_kernel,
        "project_first",
        shares + [partial],
        [half_shape, half_shape, pltpu.VMEM((width, rank), BF16)],
        [pltpu.VMEM((count, rank), F32)],
        work * rank,
    )

    received = half_sum = None
    for step in range(sections):
        if step > 0:
            own, send = kernel_call(
                functools.partial(next_kernel, width),
                "section_next",
                [*received, total, norms, *products],
                [half_shape, half_shape],
                [pltpu.VMEM((count, rank), F32)],
                4 * count * rank * (hidden + rank),
            )
        chip_sum = add([own, swap(send, "tensor", 1)])
        terms = [chip_sum] + [swap(chip_sum, "tensor", 2 * m) for m in range(1, chips)]
        if step == 0:
            terms[0], *products = kernel_call(
                enter_kernel,
                "enter",
                [chip_sum, bases, gain, gate, embedded],
                [
                    half_shape,
                    pltpu.VMEM((count, rank), F32),
                    pltpu.VMEM((rank, rank), BF16),
                    pltpu.VMEM((rank, rank), BF16),
                    pltpu.VMEM((rank, hidden), BF16),
                ],
                [pltpu.VMEM((rank, hidden), F32), pltpu.VMEM((rank, rank), F32)],
                2 * rank * width * (hidden + rank + count),
            )
        half_sum = add(terms) if step == 0 else choose(step, half_sum, terms)
        if step + 1 < sections:
            straight, crossed = onward(half_sum, 0), onward(half_sum, 1)
            if step == 0:
                half_sum, out = kernel_call(
                    leave_kernel,
                    "leave",
                    [half_sum, bases, down],
                    [half_shape, pltpu.VMEM((hidden, rank), BF16)],
                    [pltpu.VMEM((hidden, rank), F32)],
                    2 * hidden * width * rank,
                )
                products += [out]
                straight, half_sum = lax.optimization_barrier((straight, half_sum))
            handed = add([straight, crossed])
            received = [handed, swap(handed, "tensor", 1)]
    result = add([half_sum, swap(half_sum, "segment", 1)])
    (collected,) = kernel_call(
        collect_kernel,
        "collect",
        [result, swap(result, "tensor", 1)],
        [jax.ShapeDtypeStruct((1, count, rank), BF16)],
        [],
        0,
        2,
    )
    return collected


def solution(mesh):
    placed = (
        P(),
        P("segment", "tensor"),
        P(),
        P("segment", None, "tensor"),
        P("segment", "tensor", None),
        P("tensor", None),
    )
    return jax.shard_map(
        per_device, mesh=mesh, in_specs=placed, out_specs=P("segment", None, None), check_vma=False
    )
```

```python
import functools

import jax
import jax.numpy as jnp
from jax import lax
from jax.experimental import pallas as pl
from jax.experimental.pallas import tpu as pltpu
from jax.sharding import PartitionSpec as P

EPSILON = 1e-05
GROUP = 4
TILE = 16
PARTS = 8
CHUNK = 512
F32 = jnp.float32
BF16 = jnp.bfloat16


def swap(value, axis, mask):
    return lax.ppermute(value, axis, [(i, i ^ mask) for i in range(lax.axis_size(axis))])


def onward(value, flip):
    size = lax.axis_size("segment")
    return lax.ppermute(value, "segment", [(i, (i ^ flip) + 2) for i in range(size - 2)])


def tree_sum(values):
    while len(values) > 1:
        values = [values[i] + values[i + 1] for i in range(0, len(values), 2)]
    return values[0]


def split_copies(source, target, sems):
    rows = source.shape[0]
    parts = max(p for p in range(1, PARTS + 1) if rows % (TILE * p) == 0)
    size = rows // parts
    return [
        pltpu.make_async_copy(
            source.at[pl.ds(k * size, size), :], target.at[pl.ds(k * size, size), :], sems.at[k]
        )
        for k in range(parts)
    ]


def fetch_kernel(block_rows, vocab, tokens_smem, tokens_row, table, gate, *refs):
    outs, (near_gate, buffer, sem, weight_sems) = refs[:GROUP], refs[GROUP:]
    weights = split_copies(gate.at[0], near_gate, weight_sems)
    segment = lax.axis_index("segment")
    low = segment * vocab
    count = GROUP * block_rows

    def held(i):
        local = tokens_smem[i] - low
        return local, (local >= 0) & (local < vocab)

    def copy(i, local):
        first = pl.multiple_of((local // TILE) * TILE, TILE)
        place = pl.multiple_of(i * TILE, TILE)
        return pltpu.make_async_copy(
            table.at[pl.ds(first, TILE), :], buffer.at[pl.ds(place, TILE), :], sem
        )

    def start(i, started):
        local, here = held(i)

        @pl.when(here)
        def _():
            copy(i, local).start()

        return started + here.astype(jnp.int32)

    def finish(i, carry):
        copy(0, 0).wait()
        return carry

    buffer[...] = jnp.zeros_like(buffer)
    for weight in weights:
        weight.start()
    started = lax.fori_loop(0, count, start, jnp.int32(0), unroll=8)
    wanted = tokens_row[...] - low
    inside = (wanted >= 0) & (wanted < vocab)
    code = jnp.where(inside, lax.rem(wanted, TILE), TILE)
    rows = lax.broadcasted_iota(jnp.int32, (count, count), 0)
    columns = lax.broadcasted_iota(jnp.int32, (count, count), 1)
    code_column = jnp.sum(jnp.where(rows == columns, code, 0), axis=1, keepdims=True)
    lax.fori_loop(0, started, finish, 0)
    home = lax.rem(segment, GROUP)
    wide = block_rows * TILE
    row_of = lax.broadcasted_iota(jnp.int32, (block_rows, wide), 0)
    lane_of = lax.broadcasted_iota(jnp.int32, (block_rows, wide), 1)
    results = []
    for block in range(GROUP):
        code_block = code_column[block * block_rows : (block + 1) * block_rows]
        hot = (lane_of == row_of * TILE + code_block) & (code_block < TILE)
        hot = jnp.where(hot, 1.0, 0.0).astype(BF16)
        results.append(
            jnp.dot(
                hot, buffer[block * wide : (block + 1) * wide, :], preferred_element_type=F32
            ).astype(BF16)
        )
    for block in range(GROUP):
        for mask in range(GROUP):

            @pl.when(jnp.bitwise_xor(home, mask) == block)
            def _(block=block, mask=mask):
                outs[mask][...] = results[block]
    for weight in weights:
        weight.wait()


def load_kernel(gate, near_gate, sems):
    copies = split_copies(gate.at[0], near_gate, sems)
    for copy in copies:
        copy.start()
    for copy in copies:
        copy.wait()


def fetch_rows(tokens, embedding, gate):
    vocab, features = embedding.shape
    block_rows = tokens.shape[0] // GROUP
    vmem = pl.BlockSpec(memory_space=pltpu.VMEM)
    anywhere = pl.BlockSpec(memory_space=pl.ANY)
    near = pltpu.VMEM(gate.shape[1:], BF16)
    weight_sems = pltpu.SemaphoreType.DMA((PARTS,))
    params = pltpu.CompilerParams(vmem_limit_bytes=44 * 2**20)
    if vocab % TILE:
        segment = lax.axis_index("segment")
        local = tokens - segment * vocab
        inside = (local >= 0) & (local < vocab)
        picked = jnp.take(embedding, jnp.clip(local, 0, vocab - 1), axis=0)
        picked = jnp.where(inside[:, None], picked, jnp.zeros_like(picked))
        picked = picked.reshape(GROUP, block_rows, features)
        home = segment % GROUP
        blocks = [lax.dynamic_index_in_dim(picked, home ^ m, 0, False) for m in range(GROUP)]
        near = pl.pallas_call(
            load_kernel,
            out_shape=near,
            in_specs=[anywhere],
            out_specs=vmem,
            scratch_shapes=[weight_sems],
            compiler_params=params,
            name="load_weights",
        )(gate)
        return blocks, near
    *blocks, near_gate = pl.pallas_call(
        functools.partial(fetch_kernel, block_rows, vocab),
        out_shape=[jax.ShapeDtypeStruct((block_rows, features), BF16)] * GROUP + [near],
        in_specs=[pl.BlockSpec(memory_space=pltpu.SMEM), vmem] + [anywhere] * 2,
        out_specs=[vmem] * (GROUP + 1),
        scratch_shapes=[
            pltpu.VMEM((tokens.shape[0] * TILE, features), BF16),
            pltpu.SemaphoreType.DMA,
            weight_sems,
        ],
        compiler_params=params,
        name="fetch_rows",
    )(tokens, tokens.reshape(1, -1), embedding, gate)
    return blocks, near_gate


def position(chips):
    place = lax.axis_index("tensor")
    segment = lax.axis_index("segment")
    core = lax.rem(place, 2)
    chip = place // 2

    def share(side, turn):
        return jnp.bitwise_xor(chip, turn) * 2 + jnp.bitwise_xor(core, side)

    return segment, place, core, share


def first_kernel(chips, *refs):
    pieces, refs = refs[: 2 * GROUP], refs[2 * GROUP :]
    gain, gate, far_down, partial, embedded, total, norms, down, sems = refs
    copies = split_copies(far_down.at[0], down, sems)
    for copy in copies:
        copy.start()
    tokens, width = embedded.shape
    segment, place, core, share = position(chips)
    features = width // (2 * chips)
    rows = tokens // GROUP
    home = lax.rem(segment, GROUP)
    chunks = width // CHUNK
    for side in range(2):
        for turn in range(chips):
            column = pl.multiple_of(share(side, turn) * features, features)
            for block in range(GROUP):
                row = pl.multiple_of(jnp.bitwise_xor(home, block) * rows, rows)
                embedded[pl.ds(row, rows), pl.ds(column, features)] = pieces[side * GROUP + block][turn]
    gain_row = gain[pl.ds(segment // 2, 1), :]
    squares = jnp.zeros((tokens, 1), F32)
    for k in range(chunks):
        span = slice(k * CHUNK, (k + 1) * CHUNK)
        wide = embedded[:, span].astype(F32)
        squares = squares + jnp.sum(wide * wide, axis=1, keepdims=True)
        scaled = (wide * gain_row[:, span]).astype(BF16)
        product = jnp.dot(scaled, gate[span, :], preferred_element_type=F32)
        total[...] = product if k == 0 else total[...] + product
    norms[...] = squares
    for copy in copies:
        copy.wait()

    @pl.when(segment < 2)
    def _():
        inverse_norm = lax.rsqrt(squares / width + EPSILON)
        activation = jax.nn.silu(total[...] * inverse_norm).astype(BF16)
        for k in range(chunks):
            span = slice(k * CHUNK, (k + 1) * CHUNK)
            product = jnp.dot(activation, down[:, span], preferred_element_type=F32)
            partial[:, span] = product.astype(BF16)


def halves(projected, core, own, send):
    half = projected.shape[0] // 2
    own[...] = projected[pl.ds(pl.multiple_of(core * half, half), half), :].astype(BF16)
    send[...] = projected[pl.ds(pl.multiple_of((1 - core) * half, half), half), :].astype(BF16)


def project_kernel(chips, *refs):
    shares, refs = refs[: 2 * GROUP + 2], refs[2 * GROUP + 2 :]
    partial, own, send, bases, projected = refs
    width, rank = bases.shape
    segment, place, core, share = position(chips)
    features = width // (2 * chips)
    part = features // GROUP
    home = lax.rem(segment, GROUP)
    chunks = width // CHUNK
    for side in range(2):
        for turn in range(chips):
            for block in range(GROUP):
                row = share(side, turn) * features + jnp.bitwise_xor(home, block) * part
                piece, index = side * (GROUP + 1) + block, turn
                if block == GROUP - 1 and turn >= chips // 2:
                    piece, index = piece + 1, turn - chips // 2
                bases[pl.ds(pl.multiple_of(row, part), part), :] = shares[piece][index]

    @pl.when(segment < 2)
    def _():
        for k in range(chunks):
            span = slice(k * CHUNK, (k + 1) * CHUNK)
            product = jnp.dot(partial[:, span], bases[span, :], preferred_element_type=F32)
            projected[...] = product if k == 0 else projected[...] + product
        halves(projected, core, own, send)


def enter_kernel(chips, *refs):
    after, bases, gain, gate, embedded, through, seen, high, low, into, into_sum, square = refs
    segment, place, core, share = position(chips)
    through[...] = after[...]

    @pl.when(segment >= 2)
    def _():
        gain_row = gain[pl.ds(segment // 2, 1), :]
        for k in range(bases.shape[0] // CHUNK):
            span = slice(k * CHUNK, (k + 1) * CHUNK)
            table = bases[span, :]
            turned = table.astype(F32).T
            scaled = (turned * gain_row[:, span]).astype(BF16)
            products = [
                jnp.dot(scaled, gate[span, :], preferred_element_type=F32),
                jnp.dot(turned.astype(BF16), table, preferred_element_type=F32),
                jnp.dot(embedded[:, span], table, preferred_element_type=F32),
            ]
            for target, product in zip((into_sum, square, seen), products):
                target[...] = product if k == 0 else target[...] + product
        into[...] = into_sum[...].astype(BF16)
        coarse = square[...].astype(BF16)
        high[...] = coarse
        low[...] = (square[...] - coarse.astype(F32)).astype(BF16)


def leave_kernel(chips, after, bases, down, through, out, out_sum):
    segment, place, core, share = position(chips)
    through[...] = after[...]

    @pl.when(segment >= 2)
    def _():
        for k in range(bases.shape[0] // CHUNK):
            span = slice(k * CHUNK, (k + 1) * CHUNK)
            product = jnp.dot(down[:, span], bases[span, :], preferred_element_type=F32)
            out_sum[...] = product if k == 0 else out_sum[...] + product
        out[...] = out_sum[...].astype(BF16)


def sum_kernel(chips, *refs):
    *terms, total = refs
    total[...] = tree_sum([term[...].astype(F32) for term in terms]).astype(BF16)


def choose_kernel(step, chips, half_sum, *refs):
    *terms, chosen = refs

    @pl.when(lax.axis_index("segment") // 2 < step)
    def _():
        chosen[...] = half_sum[...]

    @pl.when(lax.axis_index("segment") // 2 >= step)
    def _():
        chosen[...] = tree_sum([term[...].astype(F32) for term in terms]).astype(BF16)


def collect_kernel(chips, near, far, collected):
    half = collected.shape[1] // 2
    segment, place, core, share = position(chips)
    collected[0, pl.ds(pl.multiple_of(core * half, half), half), :] = near[...]
    collected[0, pl.ds(pl.multiple_of((1 - core) * half, half), half), :] = far[...]


def next_kernel(width, chips, *refs):
    half_own, half_other, total, norms, seen, high, low, into, out, own, send, projected = refs
    segment, place, core, share = position(chips)
    upper = jnp.where(core == 0, half_own[...], half_other[...])
    lower = jnp.where(core == 0, half_other[...], half_own[...])
    received = jnp.concatenate([upper, lower], axis=0)
    rebuilt = jnp.dot(received, high[...], preferred_element_type=F32) + jnp.dot(
        received, low[...], preferred_element_type=F32
    )
    cross = received.astype(F32) * (2.0 * seen[...] + rebuilt)
    squares = norms[...] + jnp.sum(cross, axis=1, keepdims=True)
    inverse_norm = lax.rsqrt(jnp.maximum(squares, 0.0) / width + EPSILON)
    gated = total[...] + jnp.dot(received, into[...], preferred_element_type=F32)
    activation = jax.nn.silu(gated * inverse_norm).astype(BF16)
    product = jnp.dot(activation, out[...], preferred_element_type=F32)
    alone = (lax.rem(segment, 2) == 0) & (place == 0)
    projected[...] = product + jnp.where(alone, rebuilt, jnp.zeros_like(rebuilt))
    halves(projected, core, own, send)


def kernel_call(kernel, name, inputs, outs, scratch, flops, vmem_limit=14, far=()):
    vmem = pl.BlockSpec(memory_space=pltpu.VMEM)
    return pl.pallas_call(
        functools.partial(kernel, lax.axis_size("tensor") // 2),
        out_shape=outs,
        in_specs=[vmem] * len(inputs) + [pl.BlockSpec(memory_space=pl.ANY)] * len(far),
        out_specs=[vmem] * len(outs),
        scratch_shapes=scratch,
        compiler_params=pltpu.CompilerParams(vmem_limit_bytes=vmem_limit * 2**20),
        cost_estimate=pl.CostEstimate(flops=flops, bytes_accessed=0, transcendentals=0),
        name=name,
    )(*inputs, *far)


def choose(step, half_sum, terms):
    (chosen,) = kernel_call(
        functools.partial(choose_kernel, step),
        "choose",
        [half_sum, *terms],
        [jax.ShapeDtypeStruct(half_sum.shape, BF16)],
        [],
        0,
        2,
    )
    return chosen


def add(terms):
    (total,) = kernel_call(sum_kernel, "add", terms, [jax.ShapeDtypeStruct(terms[0].shape, BF16)], [], 0, 2)
    return total


def per_device(tokens, embedding, gain, gate_weight, down_weight, basis):
    segments = lax.axis_size("segment")
    chips = lax.axis_size("tensor") // 2
    sections = segments // 2
    count = tokens.shape[0]
    rank = basis.shape[1]
    width, hidden = gate_weight.shape[1:]

    home = lax.axis_index("segment") % GROUP
    part = basis.shape[0] // GROUP
    quarter = lax.dynamic_slice_in_dim(basis, home * part, part, 0)
    bands = [quarter] + [swap(quarter, "tensor", 2 * m) for m in range(1, chips)]
    blocks, gate = fetch_rows(tokens, embedding, gate_weight)
    blocks, bands[2] = lax.optimization_barrier((blocks, bands[2]))
    bands = jnp.stack(bands)
    mask = GROUP
    while mask < segments:
        blocks = [block + swap(block, "segment", mask) for block in blocks]
        mask *= 2
    arrived = [blocks[0]] + [swap(blocks[m], "segment", m) for m in range(1, GROUP)]
    arrived[1], bands = lax.optimization_barrier((arrived[1], bands))
    complete = tree_sum(arrived)
    shares = [bands] + [swap(bands, "segment", m) for m in range(1, GROUP - 1)]
    along = jnp.stack([complete] + [swap(complete, "tensor", 2 * m) for m in range(1, chips)])
    mine = [along] + [swap(along, "segment", m) for m in range(1, GROUP)]
    mine[GROUP - 1], _ = lax.optimization_barrier((mine[GROUP - 1], shares))
    shares += [swap(shares[1][: chips // 2], "segment", 2), swap(shares[2][chips // 2 :], "segment", 1)]
    theirs = [swap(piece, "tensor", 1) for piece in mine]
    work = 2 * count * width
    partial, embedded, total, norms, down = kernel_call(
        first_kernel,
        "section_first",
        mine + theirs + [gain, gate],
        [
            pltpu.VMEM((count, width), BF16),
            pltpu.VMEM((count, width), BF16),
            pltpu.VMEM((count, hidden), F32),
            pltpu.VMEM((count, 1), F32),
            pltpu.VMEM((hidden, width), BF16),
        ],
        [pltpu.SemaphoreType.DMA((PARTS,))],
        0,
        14,
        [down_weight],
    )
    partial, shares[GROUP - 1], shares[GROUP] = lax.optimization_barrier(
        (partial, shares[GROUP - 1], shares[GROUP])
    )
    shares = shares + [swap(piece, "tensor", 1) for piece in shares]
    half_shape = jax.ShapeDtypeStruct((count // 2, rank), BF16)
    own, send, bases = kernel_call(
        project_kernel,
        "project_first",
        shares + [partial],
        [half_shape, half_shape, pltpu.VMEM((width, rank), BF16)],
        [pltpu.VMEM((count, rank), F32)],
        work * rank,
    )

    received = half_sum = None
    for step in range(sections):
        if step > 0:
            own, send = kernel_call(
                functools.partial(next_kernel, width),
                "section_next",
                [*received, total, norms, *products],
                [half_shape, half_shape],
                [pltpu.VMEM((count, rank), F32)],
                4 * count * rank * (hidden + rank),
            )
        chip_sum = add([own, swap(send, "tensor", 1)])
        terms = [chip_sum] + [swap(chip_sum, "tensor", 2 * m) for m in range(1, chips)]
        if step == 0:
            terms[0], *products = kernel_call(
                enter_kernel,
                "enter",
                [chip_sum, bases, gain, gate, embedded],
                [
                    half_shape,
                    pltpu.VMEM((count, rank), F32),
                    pltpu.VMEM((rank, rank), BF16),
                    pltpu.VMEM((rank, rank), BF16),
                    pltpu.VMEM((rank, hidden), BF16),
                ],
                [pltpu.VMEM((rank, hidden), F32), pltpu.VMEM((rank, rank), F32)],
                2 * rank * width * (hidden + rank + count),
            )
        half_sum = add(terms) if step == 0 else choose(step, half_sum, terms)
        if step + 1 < sections:
            straight, crossed = onward(half_sum, 0), onward(half_sum, 1)
            if step == 0:
                half_sum, out = kernel_call(
                    leave_kernel,
                    "leave",
                    [half_sum, bases, down],
                    [half_shape, pltpu.VMEM((hidden, rank), BF16)],
                    [pltpu.VMEM((hidden, rank), F32)],
                    2 * hidden * width * rank,
                )
                products += [out]
                straight, half_sum = lax.optimization_barrier((straight, half_sum))
            handed = add([straight, crossed])
            received = [handed, swap(handed, "tensor", 1)]
    result = add([half_sum, swap(half_sum, "segment", 1)])
    (collected,) = kernel_call(
        collect_kernel,
        "collect",
        [result, swap(result, "tensor", 1)],
        [jax.ShapeDtypeStruct((1, count, rank), BF16)],
        [],
        0,
        2,
    )
    return collected


def solution(mesh):
    placed = (
        P(),
        P("segment", "tensor"),
        P(),
        P("segment", None, "tensor"),
        P("segment", "tensor", None),
        P("tensor", None),
    )
    return jax.shard_map(
        per_device, mesh=mesh, in_specs=placed, out_specs=P("segment", None, None), check_vma=False
    )
```

```python
import functools

import jax
import jax.numpy as jnp
from jax import lax
from jax.experimental import pallas as pl
from jax.experimental.pallas import tpu as pltpu
from jax.sharding import PartitionSpec as P

EPSILON = 1e-05
GROUP = 4
TILE = 16
PARTS = 8
CHUNK = 512
F32 = jnp.float32
BF16 = jnp.bfloat16


def swap(value, axis, mask):
    return lax.ppermute(value, axis, [(i, i ^ mask) for i in range(lax.axis_size(axis))])


def onward(value, flip):
    size = lax.axis_size("segment")
    return lax.ppermute(value, "segment", [(i, (i ^ flip) + 2) for i in range(size - 2)])


def tree_sum(values):
    while len(values) > 1:
        values = [values[i] + values[i + 1] for i in range(0, len(values), 2)]
    return values[0]


def split_copies(source, target, sems):
    rows = source.shape[0]
    parts = max(p for p in range(1, PARTS + 1) if rows % (TILE * p) == 0)
    size = rows // parts
    return [
        pltpu.make_async_copy(
            source.at[pl.ds(k * size, size), :], target.at[pl.ds(k * size, size), :], sems.at[k]
        )
        for k in range(parts)
    ]


def fetch_kernel(block_rows, vocab, tokens_smem, tokens_row, table, gate, *refs):
    outs, (near_gate, buffer, sem, weight_sems) = refs[:GROUP], refs[GROUP:]
    weights = split_copies(gate.at[0], near_gate, weight_sems)
    segment = lax.axis_index("segment")
    low = segment * vocab
    count = GROUP * block_rows

    def held(i):
        local = tokens_smem[i] - low
        return local, (local >= 0) & (local < vocab)

    def copy(i, local):
        first = pl.multiple_of((local // TILE) * TILE, TILE)
        place = pl.multiple_of(i * TILE, TILE)
        return pltpu.make_async_copy(
            table.at[pl.ds(first, TILE), :], buffer.at[pl.ds(place, TILE), :], sem
        )

    def start(i, started):
        local, here = held(i)

        @pl.when(here)
        def _():
            copy(i, local).start()

        return started + here.astype(jnp.int32)

    def finish(i, carry):
        copy(0, 0).wait()
        return carry

    buffer[...] = jnp.zeros_like(buffer)
    for weight in weights:
        weight.start()
    started = lax.fori_loop(0, count, start, jnp.int32(0), unroll=8)
    wanted = tokens_row[...] - low
    inside = (wanted >= 0) & (wanted < vocab)
    code = jnp.where(inside, lax.rem(wanted, TILE), TILE)
    rows = lax.broadcasted_iota(jnp.int32, (count, count), 0)
    columns = lax.broadcasted_iota(jnp.int32, (count, count), 1)
    code_column = jnp.sum(jnp.where(rows == columns, code, 0), axis=1, keepdims=True)
    lax.fori_loop(0, started, finish, 0)
    home = lax.rem(segment, GROUP)
    wide = block_rows * TILE
    row_of = lax.broadcasted_iota(jnp.int32, (block_rows, wide), 0)
    lane_of = lax.broadcasted_iota(jnp.int32, (block_rows, wide), 1)
    results = []
    for block in range(GROUP):
        code_block = code_column[block * block_rows : (block + 1) * block_rows]
        hot = (lane_of == row_of * TILE + code_block) & (code_block < TILE)
        hot = jnp.where(hot, 1.0, 0.0).astype(BF16)
        results.append(
            jnp.dot(
                hot, buffer[block * wide : (block + 1) * wide, :], preferred_element_type=F32
            ).astype(BF16)
        )
    for block in range(GROUP):
        for mask in range(GROUP):

            @pl.when(jnp.bitwise_xor(home, mask) == block)
            def _(block=block, mask=mask):
                outs[mask][...] = results[block]
    for weight in weights:
        weight.wait()


def load_kernel(gate, near_gate, sems):
    copies = split_copies(gate.at[0], near_gate, sems)
    for copy in copies:
        copy.start()
    for copy in copies:
        copy.wait()


def fetch_rows(tokens, embedding, gate):
    vocab, features = embedding.shape
    block_rows = tokens.shape[0] // GROUP
    vmem = pl.BlockSpec(memory_space=pltpu.VMEM)
    anywhere = pl.BlockSpec(memory_space=pl.ANY)
    near = pltpu.VMEM(gate.shape[1:], BF16)
    weight_sems = pltpu.SemaphoreType.DMA((PARTS,))
    params = pltpu.CompilerParams(vmem_limit_bytes=44 * 2**20)
    if vocab % TILE:
        segment = lax.axis_index("segment")
        local = tokens - segment * vocab
        inside = (local >= 0) & (local < vocab)
        picked = jnp.take(embedding, jnp.clip(local, 0, vocab - 1), axis=0)
        picked = jnp.where(inside[:, None], picked, jnp.zeros_like(picked))
        picked = picked.reshape(GROUP, block_rows, features)
        home = segment % GROUP
        blocks = [lax.dynamic_index_in_dim(picked, home ^ m, 0, False) for m in range(GROUP)]
        near = pl.pallas_call(
            load_kernel,
            out_shape=near,
            in_specs=[anywhere],
            out_specs=vmem,
            scratch_shapes=[weight_sems],
            compiler_params=params,
            name="load_weights",
        )(gate)
        return blocks, near
    *blocks, near_gate = pl.pallas_call(
        functools.partial(fetch_kernel, block_rows, vocab),
        out_shape=[jax.ShapeDtypeStruct((block_rows, features), BF16)] * GROUP + [near],
        in_specs=[pl.BlockSpec(memory_space=pltpu.SMEM), vmem] + [anywhere] * 2,
        out_specs=[vmem] * (GROUP + 1),
        scratch_shapes=[
            pltpu.VMEM((tokens.shape[0] * TILE, features), BF16),
            pltpu.SemaphoreType.DMA,
            weight_sems,
        ],
        compiler_params=params,
        name="fetch_rows",
    )(tokens, tokens.reshape(1, -1), embedding, gate)
    return blocks, near_gate


def position(chips):
    place = lax.axis_index("tensor")
    segment = lax.axis_index("segment")
    core = lax.rem(place, 2)
    chip = place // 2

    def share(side, turn):
        return jnp.bitwise_xor(chip, turn) * 2 + jnp.bitwise_xor(core, side)

    return segment, place, core, share


def first_kernel(chips, *refs):
    pieces, refs = refs[: 2 * GROUP], refs[2 * GROUP :]
    gain, gate, far_down, partial, embedded, total, norms, down, sems = refs
    copies = split_copies(far_down.at[0], down, sems)
    for copy in copies:
        copy.start()
    tokens, width = embedded.shape
    segment, place, core, share = position(chips)
    features = width // (2 * chips)
    rows = tokens // GROUP
    home = lax.rem(segment, GROUP)
    chunks = width // CHUNK
    for side in range(2):
        for turn in range(chips):
            column = pl.multiple_of(share(side, turn) * features, features)
            for block in range(GROUP):
                row = pl.multiple_of(jnp.bitwise_xor(home, block) * rows, rows)
                embedded[pl.ds(row, rows), pl.ds(column, features)] = pieces[side * GROUP + block][turn]
    gain_row = gain[pl.ds(segment // 2, 1), :]
    squares = jnp.zeros((tokens, 1), F32)
    for k in range(chunks):
        span = slice(k * CHUNK, (k + 1) * CHUNK)
        wide = embedded[:, span].astype(F32)
        squares = squares + jnp.sum(wide * wide, axis=1, keepdims=True)
        scaled = (wide * gain_row[:, span]).astype(BF16)
        product = jnp.dot(scaled, gate[span, :], preferred_element_type=F32)
        total[...] = product if k == 0 else total[...] + product
    norms[...] = squares
    for copy in copies:
        copy.wait()

    @pl.when(segment < 2)
    def _():
        inverse_norm = lax.rsqrt(squares / width + EPSILON)
        activation = jax.nn.silu(total[...] * inverse_norm).astype(BF16)
        for k in range(chunks):
            span = slice(k * CHUNK, (k + 1) * CHUNK)
            product = jnp.dot(activation, down[:, span], preferred_element_type=F32)
            partial[:, span] = product.astype(BF16)


def halves(projected, core, own, send):
    half = projected.shape[0] // 2
    own[...] = projected[pl.ds(pl.multiple_of(core * half, half), half), :].astype(BF16)
    send[...] = projected[pl.ds(pl.multiple_of((1 - core) * half, half), half), :].astype(BF16)


def project_kernel(chips, *refs):
    shares, refs = refs[: 2 * GROUP + 2], refs[2 * GROUP + 2 :]
    partial, own, send, bases, projected = refs
    width, rank = bases.shape
    segment, place, core, share = position(chips)
    features = width // (2 * chips)
    part = features // GROUP
    home = lax.rem(segment, GROUP)
    chunks = width // CHUNK
    for side in range(2):
        for turn in range(chips):
            for block in range(GROUP):
                row = share(side, turn) * features + jnp.bitwise_xor(home, block) * part
                piece, index = side * (GROUP + 1) + block, turn
                if block == GROUP - 1 and turn >= chips // 2:
                    piece, index = piece + 1, turn - chips // 2
                bases[pl.ds(pl.multiple_of(row, part), part), :] = shares[piece][index]

    @pl.when(segment < 2)
    def _():
        for k in range(chunks):
            span = slice(k * CHUNK, (k + 1) * CHUNK)
            product = jnp.dot(partial[:, span], bases[span, :], preferred_element_type=F32)
            projected[...] = product if k == 0 else projected[...] + product
        halves(projected, core, own, send)


def enter_kernel(chips, *refs):
    after, bases, gain, gate, embedded, through, seen, high, low, into, into_sum, square = refs
    segment, place, core, share = position(chips)
    through[...] = after[...]

    @pl.when(segment >= 2)
    def _():
        gain_row = gain[pl.ds(segment // 2, 1), :]
        for k in range(bases.shape[0] // CHUNK):
            span = slice(k * CHUNK, (k + 1) * CHUNK)
            table = bases[span, :]
            turned = table.astype(F32).T
            scaled = (turned * gain_row[:, span]).astype(BF16)
            products = [
                jnp.dot(scaled, gate[span, :], preferred_element_type=F32),
                jnp.dot(turned.astype(BF16), table, preferred_element_type=F32),
                jnp.dot(embedded[:, span], table, preferred_element_type=F32),
            ]
            for target, product in zip((into_sum, square, seen), products):
                target[...] = product if k == 0 else target[...] + product
        into[...] = into_sum[...].astype(BF16)
        coarse = square[...].astype(BF16)
        high[...] = coarse
        low[...] = (square[...] - coarse.astype(F32)).astype(BF16)


def leave_kernel(chips, after, bases, down, through, out, out_sum):
    segment, place, core, share = position(chips)
    through[...] = after[...]

    @pl.when(segment >= 2)
    def _():
        for k in range(bases.shape[0] // CHUNK):
            span = slice(k * CHUNK, (k + 1) * CHUNK)
            product = jnp.dot(down[:, span], bases[span, :], preferred_element_type=F32)
            out_sum[...] = product if k == 0 else out_sum[...] + product
        out[...] = out_sum[...].astype(BF16)


def sum_kernel(chips, *refs):
    *terms, total = refs
    total[...] = tree_sum([term[...].astype(F32) for term in terms]).astype(BF16)


def choose_kernel(step, chips, half_sum, *refs):
    *terms, chosen = refs

    @pl.when(lax.axis_index("segment") // 2 < step)
    def _():
        chosen[...] = half_sum[...]

    @pl.when(lax.axis_index("segment") // 2 >= step)
    def _():
        chosen[...] = tree_sum([term[...].astype(F32) for term in terms]).astype(BF16)


def collect_kernel(chips, near, far, collected):
    half = collected.shape[1] // 2
    segment, place, core, share = position(chips)
    collected[0, pl.ds(pl.multiple_of(core * half, half), half), :] = near[...]
    collected[0, pl.ds(pl.multiple_of((1 - core) * half, half), half), :] = far[...]


def next_kernel(width, chips, *refs):
    half_own, half_other, total, norms, seen, high, low, into, out, own, send, projected = refs
    segment, place, core, share = position(chips)
    upper = jnp.where(core == 0, half_own[...], half_other[...])
    lower = jnp.where(core == 0, half_other[...], half_own[...])
    received = jnp.concatenate([upper, lower], axis=0)
    rebuilt = jnp.dot(received, high[...], preferred_element_type=F32) + jnp.dot(
        received, low[...], preferred_element_type=F32
    )
    cross = received.astype(F32) * (2.0 * seen[...] + rebuilt)
    squares = norms[...] + jnp.sum(cross, axis=1, keepdims=True)
    inverse_norm = lax.rsqrt(jnp.maximum(squares, 0.0) / width + EPSILON)
    gated = total[...] + jnp.dot(received, into[...], preferred_element_type=F32)
    activation = jax.nn.silu(gated * inverse_norm).astype(BF16)
    product = jnp.dot(activation, out[...], preferred_element_type=F32)
    alone = (lax.rem(segment, 2) == 0) & (place == 0)
    projected[...] = product + jnp.where(alone, rebuilt, jnp.zeros_like(rebuilt))
    halves(projected, core, own, send)


def kernel_call(kernel, name, inputs, outs, scratch, flops, vmem_limit=14, far=()):
    vmem = pl.BlockSpec(memory_space=pltpu.VMEM)
    return pl.pallas_call(
        functools.partial(kernel, lax.axis_size("tensor") // 2),
        out_shape=outs,
        in_specs=[vmem] * len(inputs) + [pl.BlockSpec(memory_space=pl.ANY)] * len(far),
        out_specs=[vmem] * len(outs),
        scratch_shapes=scratch,
        compiler_params=pltpu.CompilerParams(vmem_limit_bytes=vmem_limit * 2**20),
        cost_estimate=pl.CostEstimate(flops=flops, bytes_accessed=0, transcendentals=0),
        name=name,
    )(*inputs, *far)


def choose(step, half_sum, terms):
    (chosen,) = kernel_call(
        functools.partial(choose_kernel, step),
        "choose",
        [half_sum, *terms],
        [jax.ShapeDtypeStruct(half_sum.shape, BF16)],
        [],
        0,
        2,
    )
    return chosen


def add(terms):
    (total,) = kernel_call(sum_kernel, "add", terms, [jax.ShapeDtypeStruct(terms[0].shape, BF16)], [], 0, 2)
    return total


def per_device(tokens, embedding, gain, gate_weight, down_weight, basis):
    segments = lax.axis_size("segment")
    chips = lax.axis_size("tensor") // 2
    sections = segments // 2
    count = tokens.shape[0]
    rank = basis.shape[1]
    width, hidden = gate_weight.shape[1:]

    home = lax.axis_index("segment") % GROUP
    part = basis.shape[0] // GROUP
    quarter = lax.dynamic_slice_in_dim(basis, home * part, part, 0)
    bands = [quarter] + [swap(quarter, "tensor", 2 * m) for m in range(1, chips)]
    blocks, gate = fetch_rows(tokens, embedding, gate_weight)
    blocks, bands[3] = lax.optimization_barrier((blocks, bands[3]))
    bands = jnp.stack(bands)
    mask = GROUP
    while mask < segments:
        blocks = [block + swap(block, "segment", mask) for block in blocks]
        mask *= 2
    arrived = [blocks[0]] + [swap(blocks[m], "segment", m) for m in range(1, GROUP)]
    arrived[1], bands = lax.optimization_barrier((arrived[1], bands))
    complete = tree_sum(arrived)
    shares = [bands] + [swap(bands, "segment", m) for m in range(1, GROUP - 1)]
    along = jnp.stack([complete] + [swap(complete, "tensor", 2 * m) for m in range(1, chips)])
    mine = [along] + [swap(along, "segment", m) for m in range(1, GROUP)]
    mine[GROUP - 1], _ = lax.optimization_barrier((mine[GROUP - 1], shares))
    shares += [swap(shares[1][: chips // 2], "segment", 2), swap(shares[2][chips // 2 :], "segment", 1)]
    theirs = [swap(piece, "tensor", 1) for piece in mine]
    work = 2 * count * width
    partial, embedded, total, norms, down = kernel_call(
        first_kernel,
        "section_first",
        mine + theirs + [gain, gate],
        [
            pltpu.VMEM((count, width), BF16),
            pltpu.VMEM((count, width), BF16),
            pltpu.VMEM((count, hidden), F32),
            pltpu.VMEM((count, 1), F32),
            pltpu.VMEM((hidden, width), BF16),
        ],
        [pltpu.SemaphoreType.DMA((PARTS,))],
        0,
        14,
        [down_weight],
    )
    partial, shares[GROUP - 1], shares[GROUP] = lax.optimization_barrier(
        (partial, shares[GROUP - 1], shares[GROUP])
    )
    shares = shares + [swap(piece, "tensor", 1) for piece in shares]
    half_shape = jax.ShapeDtypeStruct((count // 2, rank), BF16)
    own, send, bases = kernel_call(
        project_kernel,
        "project_first",
        shares + [partial],
        [half_shape, half_shape, pltpu.VMEM((width, rank), BF16)],
        [pltpu.VMEM((count, rank), F32)],
        work * rank,
    )

    received = half_sum = None
    for step in range(sections):
        if step > 0:
            own, send = kernel_call(
                functools.partial(next_kernel, width),
                "section_next",
                [*received, total, norms, *products],
                [half_shape, half_shape],
                [pltpu.VMEM((count, rank), F32)],
                4 * count * rank * (hidden + rank),
            )
        chip_sum = add([own, swap(send, "tensor", 1)])
        terms = [chip_sum] + [swap(chip_sum, "tensor", 2 * m) for m in range(1, chips)]
        if step == 0:
            terms[0], *products = kernel_call(
                enter_kernel,
                "enter",
                [chip_sum, bases, gain, gate, embedded],
                [
                    half_shape,
                    pltpu.VMEM((count, rank), F32),
                    pltpu.VMEM((rank, rank), BF16),
                    pltpu.VMEM((rank, rank), BF16),
                    pltpu.VMEM((rank, hidden), BF16),
                ],
                [pltpu.VMEM((rank, hidden), F32), pltpu.VMEM((rank, rank), F32)],
                2 * rank * width * (hidden + rank + count),
            )
        half_sum = add(terms) if step == 0 else choose(step, half_sum, terms)
        if step + 1 < sections:
            straight, crossed = onward(half_sum, 0), onward(half_sum, 1)
            if step == 0:
                half_sum, out = kernel_call(
                    leave_kernel,
                    "leave",
                    [half_sum, bases, down],
                    [half_shape, pltpu.VMEM((hidden, rank), BF16)],
                    [pltpu.VMEM((hidden, rank), F32)],
                    2 * hidden * width * rank,
                )
                products += [out]
                straight, half_sum = lax.optimization_barrier((straight, half_sum))
            handed = add([straight, crossed])
            received = [handed, swap(handed, "tensor", 1)]
    result = add([half_sum, swap(half_sum, "segment", 1)])
    (collected,) = kernel_call(
        collect_kernel,
        "collect",
        [result, swap(result, "tensor", 1)],
        [jax.ShapeDtypeStruct((1, count, rank), BF16)],
        [],
        0,
        2,
    )
    return collected


def solution(mesh):
    placed = (
        P(),
        P("segment", "tensor"),
        P(),
        P("segment", None, "tensor"),
        P("segment", "tensor", None),
        P("tensor", None),
    )
    return jax.shard_map(
        per_device, mesh=mesh, in_specs=placed, out_specs=P("segment", None, None), check_vma=False
    )
```
